32 devices in a mesh: groups: 2 (over y), fsdp: 4 (over x, core), dp: 4 (over z).
Axes of the slice: x: 2, y: 2, z: 4, core: 2. Of those that a mesh axis runs over, the one named last changes fastest.
Arguments:
- inputs: bfloat16 [4096, 8192], P(('groups', 'dp'), 'fsdp'), parts along dimension 0, may hold values from -6 to 6
- cotangent: bfloat16 [4096, 1024], P(('groups', 'dp'), 'fsdp'), parts along dimension 0, may hold values from -1.1953125 to 1.1953125
- frozen_key_weight: bfloat16 [8192, 1024], P(('fsdp', 'dp')), may hold values from -0.1875 to 0.1875
- adapter_down_weight: bfloat16 [128, 16, 8192], P(('groups', 'dp'), None, 'fsdp'), parts along dimension 0, may hold values from -0.119628906 to 0.119628906
- adapter_up_weight: bfloat16 [128, 16, 1024], P(('groups', 'dp')), parts along dimension 0, may hold values from -0.1875 to 0.1875
- row_adapter_index: int32 [4096, 1], P(('groups', 'dp')), parts along dimension 0, may hold values from 0 to 63; in each aligned block of 512 rows (0 to 511, 512 to 1023, ...) at most 16 rows name the same one
- adapter_slot_index: int32 [128], P('groups'), parts along dimension 0, may hold values from 0 to 63, each once
Outputs:
- input_grad: bfloat16 [4096, 8192], P(('groups', 'dp'), 'fsdp'), parts along dimension 0
- down_grad: bfloat16 [128, 16, 8192], P(('groups', 'dp'), None, 'fsdp'), parts along dimension 0
- up_grad: bfloat16 [128, 16, 1024], P(('groups', 'dp'), None, 'fsdp'), parts along dimension 0
The draws below stay inside these ranges and needn't reach their ends.
There are 2 independent parts, one for each index of `groups`. The reference program is written for one: setup_inputs(seed, part) draws one part's arguments, and reference() takes and returns one part's arrays. A program takes and returns all parts, laid end to end along the dimension named above; an argument that names none is the same for every part. Nothing has to cross between parts.
Inputs may be any that keep to these rules, and one draw needn't show every extreme that they name: `row_adapter_index`: among the rows of one index of dp (aligned blocks of 512 rows) no adapter is named by more than 16 rows, a bound that some block reaches. `adapter_slot_index`: a permutation: each slot holds one adapter; slot s lies on index s // 16 of dp.
All inputs are finite; a program needn't handle non-finite values.
Results may differ from the reference program's by a relative error of at most 0.005.
Values may be sent and summed in bfloat16 or wider, within the bound.
No kernel may reach another device: no remote copies, remote signals or barrier semaphores. Data moves between devices by JAX's collectives and lax.ppermute only.
A program may use at most 128 MiB of HBM per device.

```python
import math
import jax
import jax.numpy as jnp
import numpy as np
from jax import lax

MODEL_WIDTH = 8192
KEY_FEATURES = 1024
ADAPTER_RANK = 16
TOK_DEV = 512
ADAPTER_COUNT = 64
CAP = 16
TOKENS = 2048


def block_levels(own_key, dims, split, low, largest):
    loudness, own = 1.0, jax.random.fold_in(own_key, 6)
    for axis_at, blocks in split:
        steps = jnp.exp(jax.random.uniform(jax.random.fold_in(own, axis_at), (blocks,), jnp.float32, low / len(split), largest / len(split)))
        loudness = loudness * jnp.repeat(steps, dims[axis_at] // blocks).reshape([-1 if axis == axis_at else 1 for axis in range(len(dims))])
    return loudness


def routed_block(stream_key, own, number, rows, amount, top, limit, skew):
    ranking = jax.random.permutation(stream_key, amount)
    packed, common = portions_of(amount, rows * top, limit, skew, True), portions_of(amount, rows * top, limit, skew, False)
    places = jnp.arange(amount)

    def named(lengths, rotation):
        used = int((lengths > 0).sum())
        fixed = max(1, used // 4)
        shifted = fixed + (places - fixed + rotation * (used - fixed)) % max(1, amount - fixed)
        return jnp.zeros((amount,), jnp.int32).at[ranking[jnp.where(places < fixed, places, shifted)]].set(jnp.asarray(lengths, jnp.int32))

    lengths = jnp.where(number % 4 == 0, named(packed, number // 4), named(common, number - number // 4 - 1))
    mixed = jax.random.permutation(jax.random.fold_in(own, 3), amount)
    donor, taker = mixed[0:amount // 2 * 2:2], mixed[1:amount // 2 * 2:2]
    room = jnp.minimum(lengths[donor] - 1, limit - lengths[taker]) // 2
    room = jnp.where((donor == ranking[0]) | (taker == ranking[0]) | (lengths[taker] == 0), 0, jnp.maximum(room, 0))
    shifted = jax.random.randint(jax.random.fold_in(own, 4), (amount // 2,), 0, 1 << 20) % (room + 1)
    lengths = lengths.at[donor].add(-shifted).at[taker].add(shifted)
    members = jnp.searchsorted(jnp.cumsum(lengths), jnp.arange(rows * top), side="right").astype(jnp.int32)
    grid = members.reshape(top, rows).T
    grid = grid[jax.random.permutation(jax.random.fold_in(own, 1), rows)]
    rotation = jax.random.randint(jax.random.fold_in(own, 2), (rows, 1), 0, top)
    return jnp.take_along_axis(grid, (jnp.arange(top)[None, :] + rotation) % top, axis=1)


def portions_of(amount, total, reach, lean, full):
    weights = [(1 << 20) // math.isqrt(standing ** lean) + 1 for standing in range(1, amount + 1)]
    largest = reach if full else min(reach, max(-(-total // amount), total * weights[0] // sum(weights)))
    least = 1 if total - largest >= amount - 1 else 0
    given, spare = [largest] + [least] * (amount - 1), total - largest - least * (amount - 1)
    while spare > 0:
        candidates = [i for i in range(1, amount) if given[i] < largest] or [i for i in range(1, amount) if given[i] < reach]
        whole, remaining = sum([weights[i] for i in candidates]), spare
        for i in candidates:
            extra = min(reach - given[i], max(1, remaining * weights[i] // whole), spare)
            given[i] = given[i] + extra
            spare = spare - extra
    return np.array(given)


def scatter_about(own_key, extent, spread, reach, split=(), kind=jnp.bfloat16):
    entries = jax.random.normal(own_key, extent, jnp.float32) * spread
    if len(split) > 0:
        entries = block_levels(own_key, extent, split, -0.22, 0.18) * entries
    return jnp.clip(entries, min=-reach, max=reach).astype(kind)


def setup_inputs(seed: int = 0, part: int = 0) -> dict:
    splits = jax.random.split(jax.random.key(seed), 8)
    part_keys = jax.random.split(jax.random.fold_in(splits[7], part), 8)
    inputs = scatter_about(part_keys[0], (TOKENS, MODEL_WIDTH), 1.0, 6.0, ((0, 4), (1, 4)))
    cotangent = scatter_about(part_keys[1], (TOKENS, KEY_FEATURES), 0.2, 1.1953125, ((0, 4), (1, 4)))
    frozen_key_weight = scatter_about(splits[2], (MODEL_WIDTH, KEY_FEATURES), KEY_FEATURES ** -0.5, 0.1875, ((0, 16),))
    adapter_down_weight = scatter_about(part_keys[3], (ADAPTER_COUNT, ADAPTER_RANK, MODEL_WIDTH), 0.02, 0.119628906, ((0, 4), (2, 4)))
    adapter_up_weight = scatter_about(part_keys[4], (ADAPTER_COUNT, ADAPTER_RANK, KEY_FEATURES), KEY_FEATURES ** -0.5, 0.1875, ((0, 4),))
    row_adapter_index_keys = jax.random.split(jax.random.fold_in(part_keys[5], 1), TOKENS // TOK_DEV)
    row_adapter_index_turns = jax.random.permutation(jax.random.fold_in(part_keys[5], 3), TOKENS // TOK_DEV)
    row_adapter_index = jax.vmap(lambda own, number: routed_block(jax.random.fold_in(part_keys[5], 2), own, number, TOK_DEV, ADAPTER_COUNT, 1, CAP, 2))(row_adapter_index_keys, row_adapter_index_turns).reshape((TOKENS, 1))
    adapter_slot_index = jax.random.permutation(part_keys[6], ADAPTER_COUNT).astype(jnp.int32)
    return dict(inputs=inputs, cotangent=cotangent, frozen_key_weight=frozen_key_weight, adapter_down_weight=adapter_down_weight, adapter_up_weight=adapter_up_weight, row_adapter_index=row_adapter_index, adapter_slot_index=adapter_slot_index)


adapter_scale = 2.0


def reference(inputs, cotangent, frozen_key_weight, adapter_down_weight, adapter_up_weight, row_adapter_index, adapter_slot_index):
    base = jnp.dot(cotangent, frozen_key_weight.T, preferred_element_type=jnp.float32)
    slot = adapter_slot_index[row_adapter_index[:, 0]].astype(jnp.int32)
    down_gradient_total = jnp.zeros(adapter_down_weight.shape, jnp.float32)
    up_gradient_total = jnp.zeros(adapter_up_weight.shape, jnp.float32)

    def one_row(carry, item):
        down_sum, up_sum = carry
        row_in, row_dy, slot_position = item
        first_factor = lax.dynamic_index_in_dim(adapter_down_weight, slot_position, 0, False).astype(jnp.float32)
        second_factor = lax.dynamic_index_in_dim(adapter_up_weight, slot_position, 0, False).astype(jnp.float32)
        row_input_float32 = row_in.astype(jnp.float32)
        row_gradient_float32 = row_dy.astype(jnp.float32)
        key_projection = jnp.sum(first_factor * row_input_float32[None, :], axis=1).astype(jnp.bfloat16).astype(jnp.float32)
        input_backward = jnp.sum(second_factor * row_gradient_float32[None, :], axis=1).astype(jnp.bfloat16).astype(jnp.float32)
        lowrank_rows = (adapter_scale * jnp.sum(first_factor * input_backward[:, None], axis=0)).astype(jnp.bfloat16)
        previous_down = lax.dynamic_index_in_dim(down_sum, slot_position, 0, True)
        previous_up = lax.dynamic_index_in_dim(up_sum, slot_position, 0, True)
        updated_down = previous_down + adapter_scale * (input_backward[:, None] * row_input_float32[None, :])[None]
        updated_up = previous_up + adapter_scale * (key_projection[:, None] * row_gradient_float32[None, :])[None]
        down_sum = lax.dynamic_update_index_in_dim(down_sum, updated_down, slot_position, 0)
        up_sum = lax.dynamic_update_index_in_dim(up_sum, updated_up, slot_position, 0)
        return (down_sum, up_sum), lowrank_rows

    (down_gradient_total, up_gradient_total), low_rows = lax.scan(one_row, (down_gradient_total, up_gradient_total), (inputs, cotangent, slot))
    input_grad = (base + low_rows.astype(jnp.float32)).astype(jnp.bfloat16)
    return input_grad, down_gradient_total.astype(jnp.bfloat16), up_gradient_total.astype(jnp.bfloat16)
```

```python
import jax
import jax.numpy as jnp
from jax import lax
from jax.sharding import PartitionSpec as P

adapter_scale = 2.0


def dot(a, b, ca, cb):
    return lax.dot_general(a, b, (((ca,), (cb,)), ((), ())), preferred_element_type=jnp.float32)


def shards(
    inputs,
    cotangent,
    frozen_key_weight,
    adapter_down_weight,
    adapter_up_weight,
    row_adapter_index,
    adapter_slot_index,
):
    tok_rows, feat_width = inputs.shape
    key_shard = cotangent.shape[1]
    owned, rank, _ = adapter_down_weight.shape
    slots = adapter_slot_index.shape[0]
    key_at = lax.axis_index("fsdp") * key_shard

    ids = row_adapter_index[:, 0]
    every = lax.broadcasted_iota(jnp.int32, (slots, tok_rows), 0)
    slot = jnp.sum(jnp.where(ids[None, :] == every, adapter_slot_index[:, None], 0), axis=0)
    mask = (slot[None, :] == every)[:, None, :]

    def own_rows(values):
        values = values.reshape(slots, rank, tok_rows)
        part = jnp.sum(jnp.where(mask, values, 0.0), axis=0)
        return lax.psum(part, "fsdp").astype(jnp.bfloat16)

    def spread(values):
        values = (adapter_scale * values)[None]
        return jnp.where(mask, values, jnp.bfloat16(0)).reshape(slots * rank, tok_rows)

    up_own = lax.dynamic_slice_in_dim(adapter_up_weight, key_at, key_shard, 2)
    up_all = lax.all_gather(up_own.reshape(owned * rank, key_shard), "dp", axis=0, tiled=True)
    down_all = lax.all_gather(
        adapter_down_weight.reshape(owned * rank, feat_width), "dp", axis=0, tiled=True
    )
    back = spread(own_rows(dot(up_all, cotangent, 1, 1)))
    down_part = dot(back, inputs, 1, 0).astype(jnp.bfloat16)
    down_grad = lax.psum_scatter(down_part, "dp", scatter_dimension=0, tiled=True)
    proj = spread(own_rows(dot(down_all, inputs, 1, 1)))
    up_part = dot(proj, cotangent, 1, 0).astype(jnp.bfloat16)
    up_grad = lax.psum_scatter(up_part, "dp", scatter_dimension=0, tiled=True)
    full_dy = lax.all_gather(cotangent, "fsdp", axis=1, tiled=True)
    weight = lax.all_gather(frozen_key_weight, "dp", axis=0, tiled=True)
    base = dot(full_dy, weight, 1, 1)
    low = dot(back, down_all, 0, 0).astype(jnp.bfloat16)
    input_grad = (base + low.astype(jnp.float32)).astype(jnp.bfloat16)
    return (
        input_grad,
        down_grad.reshape(owned, rank, feat_width),
        up_grad.reshape(owned, rank, key_shard),
    )


def solution(mesh):
    placed = (
        P(("groups", "dp"), "fsdp"),
        P(("groups", "dp"), "fsdp"),
        P(("fsdp", "dp"), None),
        P(("groups", "dp"), None, "fsdp"),
        P(("groups", "dp"), None, None),
        P(("groups", "dp"), None),
        P("groups"),
    )
    return jax.shard_map(
        shards,
        mesh=mesh,
        in_specs=placed,
        out_specs=(
            P(("groups", "dp"), "fsdp"),
            P(("groups", "dp"), None, "fsdp"),
            P(("groups", "dp"), None, "fsdp"),
        ),
        check_vma=False,
    )
```

```python
import jax
import jax.numpy as jnp
from jax import lax
from jax.sharding import PartitionSpec as P

adapter_scale = 2.0


def dot(a, b, ca, cb):
    return lax.dot_general(a, b, (((ca,), (cb,)), ((), ())), preferred_element_type=jnp.float32)


def narrow(values):
    return values.astype(jnp.bfloat16)


def turns(value, axis):
    count = lax.axis_size(axis)
    return [
        lax.ppermute(value, axis, [(i, (i + step) % count) for i in range(count)])
        for step in range(1, count)
    ]


def add_over(value, axis):
    for other in turns(value, axis):
        value = value + other
    return value


def line_steps(value, axis):
    count = lax.axis_size(axis)
    below = above = value
    for step in range(1, count):
        below = lax.ppermute(below, axis, [(i, i + 1) for i in range(step - 1, count - 1)])
        above = lax.ppermute(above, axis, [(i + 1, i) for i in range(count - step)])
        yield step, below, above


def line_pieces(value, axis):
    count, place = lax.axis_size(axis), lax.axis_index(axis)
    for step, below, above in line_steps(value, axis):
        if 2 * step < count:
            yield place - step, below
            yield place + step, above
        else:
            yield jnp.where(place < count - step, place + step, place - step), below + above


def line_sums(part, axis):
    count, place = lax.axis_size(axis), lax.axis_index(axis)
    below = above = 0.0
    for step in range(1, count):
        far = count - step
        up = [(i, i + 1) for i in range(step)]
        down = [(i, i - 1) for i in range(far, count)]
        if 2 * step <= count:
            sent = narrow(part(jnp.where(place < step, place + far, place - far)) + below + above)
            if 2 * step < count - 1:
                below, above = lax.ppermute(sent, axis, up + down), 0.0
            else:
                below, above = lax.ppermute(sent, axis, up), lax.ppermute(sent, axis, down)
        else:
            to_up = narrow(part(place + far) + below)
            to_down = narrow(part(place - far) + above)
            below, above = lax.ppermute(to_up, axis, up), lax.ppermute(to_down, axis, down)
    return narrow(part(place) + below + above)


def shards(
    inputs,
    cotangent,
    frozen_key_weight,
    adapter_down_weight,
    adapter_up_weight,
    row_adapter_index,
    adapter_slot_index,
):
    tok_rows, feat_width = inputs.shape
    key_shard = cotangent.shape[1]
    owned, rank, _ = adapter_down_weight.shape
    slots = adapter_slot_index.shape[0]
    data_count, place = lax.axis_size("dp"), lax.axis_index("dp")
    weight_rows, key_width = frozen_key_weight.shape
    groups, group = lax.axis_size("groups"), lax.axis_index("groups")
    key_at = lax.axis_index("fsdp") * key_shard

    ids = row_adapter_index[:, 0]
    every = lax.broadcasted_iota(jnp.int32, (slots, tok_rows), 0)
    slot = jnp.sum(jnp.where(ids[None, :] == every, adapter_slot_index[:, None], 0), axis=0)
    owned_at = lax.broadcasted_iota(jnp.int32, (owned, tok_rows), 0)

    def named(block):
        return (slot[None, :] - block * owned == owned_at)[:, None, :]

    def pick(block, values):
        values = values.reshape(owned, rank, tok_rows)
        return jnp.sum(jnp.where(named(block), values, 0.0), axis=0)

    def spread(block, values):
        return jnp.where(named(block), values[None], jnp.bfloat16(0)).reshape(owned * rank, tok_rows)

    up_own = lax.dynamic_slice_in_dim(adapter_up_weight, key_at, key_shard, 2)
    up_own = up_own.reshape(owned * rank, key_shard)
    up_parts = [up_own] + turns(up_own, "dp")
    down_own = adapter_down_weight.reshape(owned * rank, feat_width)
    full_dy = lax.all_gather(cotangent, "fsdp", axis=1, tiled=True)

    back = sum(
        pick((place - turn) % data_count, dot(part, cotangent, 1, 1))
        for turn, part in enumerate(up_parts)
    )
    back = adapter_scale * narrow(add_over(back, "fsdp"))

    margin = (data_count - 1) // 2
    gathered = data_count + 2 * margin

    def put(whole, block, piece, within=0):
        return lax.dynamic_update_slice(
            whole, piece[None, None], (block + margin, within, 0, 0)
        )

    down_all = jnp.zeros((gathered, 1, owned * rank, feat_width), jnp.bfloat16)
    down_all = put(down_all, place, down_own)
    proj = pick(place, dot(down_own, inputs, 1, 1))
    for block, piece in line_pieces(down_own, "dp"):
        proj = proj + pick(block, dot(piece, inputs, 1, 1))
        down_all = put(down_all, block, piece)

    half_rows = weight_rows // groups
    halves = frozen_key_weight.reshape(groups, half_rows, key_width)
    weight = jnp.zeros((gathered, groups, half_rows, key_width), jnp.bfloat16)
    weight = lax.dynamic_update_slice(weight, halves[None], (place + margin, 0, 0, 0))
    mine = lax.dynamic_index_in_dim(halves, group, 0, False)
    for block, piece in line_pieces(mine, "dp"):
        weight = put(weight, block, piece, group)
        for turn, other in enumerate(turns(piece, "groups")):
            weight = put(weight, block, other, (group - turn - 1) % groups)

    down_grad = line_sums(lambda block: dot(spread(block, back), inputs, 1, 0), "dp")

    proj = adapter_scale * narrow(add_over(proj, "fsdp"))

    def up_part(block):
        return dot(spread(block, proj), cotangent, 1, 0)

    up_grad = up_part(place)
    for turn in range(1, data_count):
        pairs = [(i, (i + turn) % data_count) for i in range(data_count)]
        up_grad = up_grad + lax.ppermute(narrow(up_part((place + turn) % data_count)), "dp", pairs)

    def whole(array):
        return array[margin : margin + data_count].reshape(-1, array.shape[-1])

    every_back = jnp.concatenate([spread(block, back) for block in range(data_count)], axis=0)
    low = narrow(dot(every_back, whole(down_all), 0, 0))
    base = dot(full_dy, whole(weight), 1, 1)
    input_grad = narrow(base + low.astype(jnp.float32))
    return (
        input_grad,
        down_grad.reshape(owned, rank, feat_width),
        narrow(up_grad).reshape(owned, rank, key_shard),
    )


def solution(mesh):
    placed = (
        P(("groups", "dp"), "fsdp"),
        P(("groups", "dp"), "fsdp"),
        P(("fsdp", "dp"), None),
        P(("groups", "dp"), None, "fsdp"),
        P(("groups", "dp"), None, None),
        P(("groups", "dp"), None),
        P("groups"),
    )
    return jax.shard_map(
        shards,
        mesh=mesh,
        in_specs=placed,
        out_specs=(
            P(("groups", "dp"), "fsdp"),
            P(("groups", "dp"), None, "fsdp"),
            P(("groups", "dp"), None, "fsdp"),
        ),
        check_vma=False,
    )
```

```python
import functools

import jax
import jax.numpy as jnp
from jax import lax
from jax.experimental import pallas as pl
from jax.experimental.pallas import tpu as pltpu
from jax.sharding import PartitionSpec as P

adapter_scale = 2.0
vmem_bytes = 24 * 1024 * 1024


def dot(a, b, ca, cb):
    return lax.dot_general(a, b, (((ca,), (cb,)), ((), ())), preferred_element_type=jnp.float32)


def narrow(values):
    return values.astype(jnp.bfloat16)


def turns(value, axis):
    count = lax.axis_size(axis)
    return [
        lax.ppermute(value, axis, [(i, (i + step) % count) for i in range(count)])
        for step in range(1, count)
    ]


def halving(value, axis):
    count = lax.axis_size(axis)
    if count & (count - 1):
        return [value] + turns(value, axis)
    step = 1
    while True:
        other = lax.ppermute(value, axis, [(i, i ^ step) for i in range(count)])
        step *= 2
        if step >= count:
            return [value, other]
        value = value + other


def after(value, *others):
    return lax.optimization_barrier((value, others))[0]


def halving(value, axis):
    count = lax.axis_size(axis)
    if count & (count - 1):
        return [value] + turns(value, axis)
    step = 1
    while True:
        other = lax.ppermute(value, axis, [(i, i ^ step) for i in range(count)])
        step *= 2
        if step >= count:
            return [value, other]
        value = value + other


def after(value, *others):
    return lax.optimization_barrier((value, others))[0]


def line_pass(below, above, axis, step):
    count = lax.axis_size(axis)
    up = [(i, i + 1) for i in range(step - 1, count - 1)]
    down = [(i + 1, i) for i in range(count - step)]
    return lax.ppermute(below, axis, up), lax.ppermute(above, axis, down)


def pairs(count, odd):
    swaps = [(i, i + 1) for i in range(odd, count - 1, 2)]
    return swaps + [(b, a) for a, b in swaps]


def going_up(place, odd):
    return lax.rem(place, 2) == odd


def arrived(count, place, step, odd):
    return jnp.where(going_up(place, odd), place + step, place - step)


def within(count, block):
    return (block >= 0) & (block < count)


def one_sided(count, step):
    return 2 * step >= count


def only_sums(count, step, odd):
    return step >= count - odd


def only_blocks(step, odd):
    return step <= 1 + odd


def named(slot, block, owned, rank):
    shape = (owned * rank, slot.shape[1])
    return (slot - block * owned) == lax.broadcasted_iota(jnp.int32, shape, 0) // rank


def pick(slot, block, values, owned, rank):
    values = jnp.where(named(slot, block, owned, rank), values, 0.0)
    total = values[:rank]
    for at in range(1, owned):
        total = total + values[at * rank : (at + 1) * rank]
    return total


def spread(slot, block, values, owned, rank):
    values = jnp.concatenate([values.astype(jnp.float32)] * owned, axis=0)
    return narrow(jnp.where(named(slot, block, owned, rank), values, 0.0))


def full(shape):
    return pl.BlockSpec(shape, lambda *at: (0,) * len(shape))


def call(body, grid, in_specs, out_specs, out_shape, *operands):
    return pl.pallas_call(
        body,
        grid=grid,
        in_specs=in_specs,
        out_specs=out_specs,
        out_shape=out_shape,
        compiler_params=pltpu.CompilerParams(vmem_limit_bytes=vmem_bytes),
        cost_estimate=pl.CostEstimate(flops=1, bytes_accessed=1, transcendentals=0),
    )(*operands)


def back_sum(slot, cotangent, parts, owned, rank):
    count, rows = len(parts), slot.shape[1]

    def body(slot_ref, cot_ref, *refs):
        place = lax.axis_index("dp")
        slots, cots = slot_ref[...], cot_ref[...]
        total = jnp.zeros((rank, rows), jnp.float32)
        for turn in range(count):
            block = lax.rem(place + count - turn, count)
            total = total + pick(slots, block, dot(refs[turn][...], cots, 1, 1), owned, rank)
        refs[count][...] = total

    return call(
        body,
        (1,),
        [full(slot.shape), full(cotangent.shape)] + [full(part.shape) for part in parts],
        full((rank, rows)),
        jax.ShapeDtypeStruct((rank, rows), jnp.float32),
        slot,
        cotangent,
        *parts,
    )


def scaled_sum(parts):
    def body(*refs):
        total = refs[0][...]
        for ref in refs[1:-1]:
            total = total + ref[...]
        refs[-1][...] = narrow(adapter_scale * narrow(total).astype(jnp.float32))

    shape = parts[0].shape
    return call(
        body,
        (1,),
        [full(shape)] * len(parts),
        full(shape),
        jax.ShapeDtypeStruct(shape, jnp.bfloat16),
        *parts,
    )


def message(step, count, odd, slot, back, inputs, received, owned, rank):
    rows, width = inputs.shape
    tile = 512 if width % 512 == 0 else width
    down_rows = owned * rank
    height = down_rows if only_sums(count, step, odd) else received.shape[0]

    def body(slot_ref, back_ref, in_ref, got_ref, out_ref):
        place = lax.axis_index("dp")
        up = going_up(place, odd)
        along = jnp.where(up, place, count - 1 - place)

        def add():
            target = along + count - step + 1
            block = jnp.where(up, target, count - 1 - target)
            factor = spread(slot_ref[...], block, back_ref[...], owned, rank)
            value = dot(factor, in_ref[...], 1, 0) + got_ref[:down_rows, :].astype(jnp.float32)
            out_ref[:down_rows, :] = narrow(value)
            if height > down_rows:
                out_ref[down_rows:, :] = jnp.zeros((height - down_rows, tile), jnp.bfloat16)

        def pass_on():
            out_ref[...] = got_ref[...]

        if height == down_rows:
            add()
        else:
            pl.when(along < step - 1)(add)
            pl.when(along >= step - 1)(pass_on)

    def moving(height):
        return pl.BlockSpec((height, tile), lambda at: (0, at))

    return call(
        body,
        (width // tile,),
        [full(slot.shape), full(back.shape), moving(rows), moving(height)],
        moving(height),
        jax.ShapeDtypeStruct((height, width), jnp.bfloat16),
        slot,
        back,
        inputs,
        received,
    )


def own_sum(count, slot, back, inputs, received, owned, rank):
    rows, width = inputs.shape
    tile = 512 if width % 512 == 0 else width
    down_rows = owned * rank

    def body(slot_ref, back_ref, in_ref, *refs):
        factor = spread(slot_ref[...], lax.axis_index("dp"), back_ref[...], owned, rank)
        value = dot(factor, in_ref[...], 1, 0)
        for ref in refs[:-1]:
            value = value + ref[...].astype(jnp.float32)
        refs[-1][...] = narrow(value)

    def moving(height):
        return pl.BlockSpec((height, tile), lambda at: (0, at))

    return call(
        body,
        (width // tile,),
        [full(slot.shape), full(back.shape), moving(rows)] + [moving(down_rows)] * len(received),
        moving(down_rows),
        jax.ShapeDtypeStruct((down_rows, width), jnp.bfloat16),
        slot,
        back,
        inputs,
        *received,
    )


def use_pieces(step, count, slot, back, inputs, pieces, held, owned, rank):
    rows, width = inputs.shape
    tile = 512 if width % 512 == 0 else width
    down_rows = owned * rank
    total = len(pieces)
    share = pieces[0].shape[0] - down_rows
    merged = one_sided(count, step) and total > 1
    shared = share * (1 if merged else total)

    def body(slot_ref, back_ref, in_ref, *refs):
        place = lax.axis_index("dp")
        slots, backs, ins = slot_ref[...], back_ref[...], in_ref[...]
        if share:
            proj_ref, low_ref, share_ref = refs[-3:]
            share_refs = refs[total : 2 * total]
            if merged:
                even_came = within(count, arrived(count, place, step, 0))
                share_ref[...] = jnp.where(even_came, share_refs[0][...], share_refs[1][...])
            else:
                for at, ref in enumerate(share_refs):
                    share_ref[at * share : (at + 1) * share, :] = ref[...]
        else:
            proj_ref, low_ref = refs[-2:]
        proj, low = None, None
        for odd, ref in enumerate(refs[:total]):
            block = arrived(count, place, step, odd) if step else place
            value = ref[...]
            term = pick(slots, block, dot(value, ins, 1, 1), owned, rank)
            proj = term if proj is None else proj + term
            term = narrow(dot(spread(slots, block, backs, owned, rank), value, 0, 0))
            low = term if low is None else low + term
        low_ref[...] = low if held is None else low + refs[total * (2 if share else 1)][...]

        @pl.when(pl.program_id(0) == 0)
        def first():
            proj_ref[...] = proj

        @pl.when(pl.program_id(0) > 0)
        def later():
            proj_ref[...] = proj_ref[...] + proj

    def moving(height, at_row=0):
        return pl.BlockSpec((height, tile), lambda at: (at_row, at))

    return call(
        body,
        (width // tile,),
        [full(slot.shape), full(back.shape), moving(rows)]
        + [moving(down_rows)] * total
        + ([moving(share, down_rows // share)] * total if share else [])
        + ([] if held is None else [moving(rows)]),
        [full((rank, rows)), moving(rows)] + ([moving(shared)] if share else []),
        [
            jax.ShapeDtypeStruct((rank, rows), jnp.float32),
            jax.ShapeDtypeStruct((rows, width), jnp.bfloat16),
        ]
        + ([jax.ShapeDtypeStruct((shared, width), jnp.bfloat16)] if share else []),
        slot,
        back,
        inputs,
        *pieces,
        *(pieces if share else []),
        *([] if held is None else [held]),
    )


def up_parts(blocks, slot, proj, cotangent, owned, rank):
    keys = cotangent.shape[1]

    def body(block_ref, slot_ref, proj_ref, cot_ref, *outs):
        slots, projs, cots = slot_ref[...], proj_ref[...], cot_ref[...]
        for at, out in enumerate(outs):
            out[...] = narrow(dot(spread(slots, block_ref[at], projs, owned, rank), cots, 1, 0))

    shape = (owned * rank, keys)
    return call(
        body,
        (1,),
        [pl.BlockSpec(memory_space=pltpu.SMEM)]
        + [full(slot.shape), full(proj.shape), full(cotangent.shape)],
        [full(shape)] * len(blocks),
        [jax.ShapeDtypeStruct(shape, jnp.bfloat16)] * len(blocks),
        jnp.stack(blocks),
        slot,
        proj,
        cotangent,
    )


def pack(down_own, weight):
    down_rows, width = down_own.shape
    half = weight.shape[0] // lax.axis_size("groups")
    keys = weight.shape[1]
    chunks = width // keys
    chunk = half // chunks

    def body(down_ref, weight_ref, out_ref):
        group = lax.axis_index("groups")
        out_ref[:down_rows, :] = down_ref[...]
        for at in range(chunks):
            rows = pl.ds(pl.multiple_of(group * half + at * chunk, chunk), chunk)
            out_ref[down_rows:, at * keys : (at + 1) * keys] = weight_ref[rows, :]

    shape = (down_rows + chunk, width)
    return call(
        body,
        (1,),
        [full(down_own.shape), full(weight.shape)],
        full(shape),
        jax.ShapeDtypeStruct(shape, jnp.bfloat16),
        down_own,
        weight,
    )


def finish(cotangents, weight_own, steps, pieces, low):
    rows, width = low.shape
    weight_rows, keys = weight_own.shape
    shard = cotangents[0].shape[1]
    count, groups, parts = lax.axis_size("dp"), lax.axis_size("groups"), len(cotangents)
    half = weight_rows // groups
    chunks = width // keys
    chunk = half // chunks
    some = max(1, 512 // weight_rows)
    tile = some * weight_rows

    def body(*refs):
        cot_refs, own_ref, refs = refs[:parts], refs[parts], refs[parts + 1 :]
        piece_refs, (low_ref, out_ref, dy_ref, weight_ref) = refs[:-4], refs[-4:]

        @pl.when(pl.program_id(0) == 0)
        def arrange():
            place, group, part = (lax.axis_index(axis) for axis in ("dp", "groups", "fsdp"))
            for turn, ref in enumerate(cot_refs):
                at = lax.rem(part + parts - turn, parts) * shard
                dy_ref[:, pl.ds(pl.multiple_of(at, shard), shard)] = ref[...]
            weight_ref[place] = own_ref[...]
            for at, ref in enumerate(piece_refs):
                step, odds = steps[at // groups]
                owner = lax.rem(group + groups - at % groups, groups)
                for odd in odds:
                    block = arrived(count, place, step, odd)
                    number = 0 if one_sided(count, step) else odd

                    def store(number=number, block=block):
                        for part in range(chunks):
                            row = pl.multiple_of(owner * half + part * chunk, chunk)
                            weight_ref[block, pl.ds(row, chunk), :] = ref[
                                number * chunk : (number + 1) * chunk,
                                part * keys : (part + 1) * keys,
                            ]

                    pl.when(within(count, block))(store)

        for block in range(some):
            at = slice(block * weight_rows, (block + 1) * weight_rows)
            base = dot(dy_ref[...], weight_ref[pl.program_id(0) * some + block], 1, 1)
            out_ref[:, at] = narrow(base + low_ref[:, at].astype(jnp.float32))

    columns = pl.BlockSpec((rows, tile), lambda at: (0, at))
    fixed = [*cotangents, weight_own, *pieces]
    return pl.pallas_call(
        body,
        grid=(width // tile,),
        in_specs=[full(array.shape) for array in fixed] + [columns],
        out_specs=columns,
        out_shape=jax.ShapeDtypeStruct((rows, width), jnp.bfloat16),
        scratch_shapes=[
            pltpu.VMEM((rows, keys), jnp.bfloat16),
            pltpu.VMEM((count, weight_rows, keys), jnp.bfloat16),
        ],
        compiler_params=pltpu.CompilerParams(vmem_limit_bytes=vmem_bytes),
        cost_estimate=pl.CostEstimate(flops=1, bytes_accessed=1, transcendentals=0),
    )(*fixed, low)


def shards(
    inputs,
    cotangent,
    frozen_key_weight,
    adapter_down_weight,
    adapter_up_weight,
    row_adapter_index,
    adapter_slot_index,
):
    tok_rows, feat_width = inputs.shape
    key_shard = cotangent.shape[1]
    owned, rank, _ = adapter_down_weight.shape
    slots = adapter_slot_index.shape[0]
    data_count, place = lax.axis_size("dp"), lax.axis_index("dp")
    down_rows = owned * rank
    key_at = lax.axis_index("fsdp") * key_shard

    up_own = lax.dynamic_slice_in_dim(adapter_up_weight, key_at, key_shard, 2)
    up_own = up_own.reshape(down_rows, key_shard)
    ups = [up_own] + turns(up_own, "dp")
    down_own = adapter_down_weight.reshape(down_rows, feat_width)
    packed = pack(down_own, frozen_key_weight)

    ids = row_adapter_index[:, 0]
    every = lax.broadcasted_iota(jnp.int32, (slots, tok_rows), 0)
    slot = jnp.sum(jnp.where(ids[None, :] == every, adapter_slot_index[:, None], 0), axis=0)
    slot = slot[None, :]

    back = back_sum(slot, cotangent, ups, owned, rank)
    back = scaled_sum([back] + turns(back, "fsdp"))
    cotangents = [cotangent] + turns(after(cotangent, back), "fsdp")
    proj, low = use_pieces(0, data_count, slot, back, inputs, [down_own], None, owned, rank)

    def up_swaps(steps, proj):
        routes = []
        for step in steps:
            for odd in (0, 1):
                ends = [i for i in range(data_count - step) if i // step % 2 == odd]
                if ends:
                    other = jnp.where(place // step % 2 == odd, place + step, place - step)
                    swaps = [(i, i + step) for i in ends] + [(i + step, i) for i in ends]
                    routes.append((other, swaps))
        parts = up_parts(
            [place] + [other for other, _ in routes], slot, proj, cotangent, owned, rank
        )
        return parts, [lax.ppermute(part, "dp", way) for part, (_, way) in zip(parts[1:], routes)]

    early = data_count // 2
    received = [after(packed, *ups)] * 2
    steps, shares, up_grads, waited = [], [], [], [[], [cotangents]]
    for step in range(1, data_count + 1):
        sent = []
        for odd, other in enumerate(reversed(received)):
            other = after(other, waited[step - 1])
            if not only_blocks(step, odd):
                other = message(step, data_count, odd, slot, back, inputs, other, owned, rank)
            sent.append(other)
        if step > 1:
            got = after(got, sent)
            term, low, share = use_pieces(
                step - 1, data_count, slot, back, inputs, got, low, owned, rank
            )
            proj = proj + term
            share = [share] + turns(share, "groups")
            shares += share
            waited.append([low, share])
            if step - 1 == early:
                near = scaled_sum(halving(proj, "fsdp"))
                parts, up_grads = up_swaps(range(1, early + 1), near)
                up_grads.append(parts[0])
                waited[-1].append(parts)
                proj = 0.0
        received = [lax.ppermute(sent[odd], "dp", pairs(data_count, odd)) for odd in (0, 1)]
        odds = [odd for odd in (0, 1) if not only_sums(data_count, step, odd)]
        got = [received[odd] for odd in odds]
        steps.append((step, odds))

    far = scaled_sum(halving(proj, "fsdp"))
    up_grads += up_swaps(range(early + 1, data_count), far)[1]
    up_grad = sum(part.astype(jnp.float32) for part in up_grads)

    input_grad = finish(cotangents, frozen_key_weight, steps[:-1], shares, low)
    received = after(received, input_grad)
    down_grad = own_sum(data_count, slot, back, inputs, received, owned, rank)
    return (
        input_grad,
        down_grad.reshape(owned, rank, feat_width),
        narrow(up_grad).reshape(owned, rank, key_shard),
    )


def solution(mesh):
    placed = (
        P(("groups", "dp"), "fsdp"),
        P(("groups", "dp"), "fsdp"),
        P(("fsdp", "dp"), None),
        P(("groups", "dp"), None, "fsdp"),
        P(("groups", "dp"), None, None),
        P(("groups", "dp"), None),
        P("groups"),
    )
    return jax.shard_map(
        shards,
        mesh=mesh,
        in_specs=placed,
        out_specs=(
            P(("groups", "dp"), "fsdp"),
            P(("groups", "dp"), None, "fsdp"),
            P(("groups", "dp"), None, "fsdp"),
        ),
        check_vma=False,
    )
```

```python
import functools

import jax
import jax.numpy as jnp
from jax import lax
from jax.experimental import pallas as pl
from jax.experimental.pallas import tpu as pltpu
from jax.sharding import PartitionSpec as P

adapter_scale = 2.0
piece_flops = 1
vmem_bytes = 24 * 1024 * 1024


def dot(a, b, ca, cb):
    return lax.dot_general(a, b, (((ca,), (cb,)), ((), ())), preferred_element_type=jnp.float32)


def narrow(values):
    return values.astype(jnp.bfloat16)


def turns(value, axis):
    count = lax.axis_size(axis)
    return [
        lax.ppermute(value, axis, [(i, (i + step) % count) for i in range(count)])
        for step in range(1, count)
    ]


def after(value, *others):
    return lax.optimization_barrier((value, others))[0]


def halving(value, axis):
    count = lax.axis_size(axis)
    if count & (count - 1):
        return [value] + turns(value, axis)
    step = 1
    while True:
        other = lax.ppermute(value, axis, [(i, i ^ step) for i in range(count)])
        step *= 2
        if step >= count:
            return [value, other]
        value = value + other


def after(value, *others):
    return lax.optimization_barrier((value, others))[0]


def line_pass(below, above, axis, step):
    count = lax.axis_size(axis)
    up = [(i, i + 1) for i in range(step - 1, count - 1)]
    down = [(i + 1, i) for i in range(count - step)]
    return lax.ppermute(below, axis, up), lax.ppermute(above, axis, down)


def pairs(count, odd):
    swaps = [(i, i + 1) for i in range(odd, count - 1, 2)]
    return swaps + [(b, a) for a, b in swaps]


def going_up(place, odd):
    return lax.rem(place, 2) == odd


def arrived(count, place, step, odd):
    return jnp.where(going_up(place, odd), place + step, place - step)


def within(count, block):
    return (block >= 0) & (block < count)


def one_sided(count, step):
    return 2 * step >= count


def only_sums(count, step, odd):
    return step >= count - odd


def only_blocks(step, odd):
    return step <= 1 + odd


def named(slot, block, owned, rank):
    shape = (owned * rank, slot.shape[1])
    return (slot - block * owned) == lax.broadcasted_iota(jnp.int32, shape, 0) // rank


def pick(slot, block, values, owned, rank):
    values = jnp.where(named(slot, block, owned, rank), values, 0.0)
    total = values[:rank]
    for at in range(1, owned):
        total = total + values[at * rank : (at + 1) * rank]
    return total


def spread(slot, block, values, owned, rank):
    values = jnp.concatenate([values.astype(jnp.float32)] * owned, axis=0)
    return narrow(jnp.where(named(slot, block, owned, rank), values, 0.0))


def columns(height, tile, at_tile=0, at_row=0):
    return pl.BlockSpec((height, tile), lambda at: (at_row, at_tile + at))


def tile_of(width):
    return 512 if width % 512 == 0 else width


def full(shape):
    return pl.BlockSpec(shape, lambda *at: (0,) * len(shape))


def call(body, grid, in_specs, out_specs, out_shape, *operands, scratch=(), aliases=None, flops=1):
    return pl.pallas_call(
        body,
        grid=grid,
        in_specs=in_specs,
        out_specs=out_specs,
        out_shape=out_shape,
        scratch_shapes=scratch,
        input_output_aliases=aliases or {},
        compiler_params=pltpu.CompilerParams(vmem_limit_bytes=vmem_bytes),
        cost_estimate=pl.CostEstimate(flops=flops, bytes_accessed=1, transcendentals=0),
    )(*operands)


def back_sum(slot, cotangent, parts, owned, rank):
    count, rows = len(parts), slot.shape[1]

    def body(slot_ref, cot_ref, *refs):
        place = lax.axis_index("dp")
        slots, cots = slot_ref[...], cot_ref[...]
        total = jnp.zeros((rank, rows), jnp.float32)
        for turn in range(count):
            block = lax.rem(place + count - turn, count)
            total = total + pick(slots, block, dot(refs[turn][...], cots, 1, 1), owned, rank)
        refs[count][...] = total

    return call(
        body,
        (1,),
        [full(slot.shape), full(cotangent.shape)] + [full(part.shape) for part in parts],
        full((rank, rows)),
        jax.ShapeDtypeStruct((rank, rows), jnp.float32),
        slot,
        cotangent,
        *parts,
    )


def add_up(parts, last):
    def body(*refs):
        total = refs[0][...]
        for ref in refs[1:-1]:
            total = total + ref[...]
        if last:
            total = narrow(adapter_scale * narrow(total).astype(jnp.float32))
        refs[-1][...] = total

    shape = parts[0].shape
    return call(
        body,
        (1,),
        [full(shape)] * len(parts),
        full(shape),
        jax.ShapeDtypeStruct(shape, jnp.bfloat16 if last else jnp.float32),
        *parts,
    )


def scaled_sum(value, axis):
    count = lax.axis_size(axis)
    if count & (count - 1):
        return add_up([value] + turns(value, axis), True)
    step = 1
    while step < count:
        other = lax.ppermute(value, axis, [(i, i ^ step) for i in range(count)])
        step *= 2
        value = add_up([value, other], step >= count)
    return value


def message(step, count, odd, stream, slot, back, inputs, received, owned, rank):
    rows, width = inputs.shape[0], received.shape[1]
    tile = tile_of(width)
    down_rows = owned * rank
    height = down_rows if only_sums(count, step, odd) else received.shape[0]

    def body(slot_ref, back_ref, in_ref, got_ref, out_ref, factor_ref):
        place = lax.axis_index("dp")
        up = going_up(place, odd)
        along = jnp.where(up, place, count - 1 - place)
        target = along + count - step + 1
        block = jnp.where(up, target, count - 1 - target)

        @pl.when(pl.program_id(0) == 0)
        def prepare():
            factor_ref[...] = spread(slot_ref[...], block, back_ref[...], owned, rank)

        def add():
            value = dot(factor_ref[...], in_ref[...], 1, 0)
            out_ref[:down_rows, :] = narrow(value + got_ref[:down_rows, :].astype(jnp.float32))
            if height > down_rows:
                out_ref[down_rows:, :] = jnp.zeros((height - down_rows, tile), jnp.bfloat16)

        def pass_on():
            out_ref[...] = got_ref[...]

        if height == down_rows:
            add()
        else:
            pl.when(along < step - 1)(add)
            pl.when(along >= step - 1)(pass_on)

    return call(
        body,
        (width // tile,),
        [
            full(slot.shape),
            full(back.shape),
            columns(rows, tile, stream * (width // tile)),
            columns(height, tile),
        ],
        columns(height, tile),
        jax.ShapeDtypeStruct((height, width), jnp.bfloat16),
        slot,
        back,
        inputs,
        received,
        scratch=[pltpu.VMEM((down_rows, rows), jnp.bfloat16)],
    )


def own_sum(stream, slot, back, inputs, received, whole, owned, rank):
    rows, width = inputs.shape[0], received[0].shape[1]
    tile = tile_of(width)
    down_rows = owned * rank
    first = stream * (width // tile)
    given = [] if whole is None else [whole]

    def body(slot_ref, back_ref, in_ref, *refs):
        out_ref, factor_ref = refs[-2:]

        @pl.when(pl.program_id(0) == 0)
        def prepare():
            place = lax.axis_index("dp")
            factor_ref[...] = spread(slot_ref[...], place, back_ref[...], owned, rank)

        value = dot(factor_ref[...], in_ref[...], 1, 0)
        for ref in refs[: len(received)]:
            value = value + ref[...].astype(jnp.float32)
        out_ref[...] = narrow(value)

    return call(
        body,
        (width // tile,),
        [full(slot.shape), full(back.shape), columns(rows, tile, first)]
        + [columns(down_rows, tile)] * len(received)
        + [pl.BlockSpec(memory_space=pl.ANY)] * len(given),
        columns(down_rows, tile, first),
        jax.ShapeDtypeStruct((down_rows, inputs.shape[1]), jnp.bfloat16),
        slot,
        back,
        inputs,
        *received,
        *given,
        scratch=[pltpu.VMEM((down_rows, rows), jnp.bfloat16)],
        aliases={3 + len(received): 0} if given else None,
    )


def use_pieces(step, count, stream, slot, back, inputs, pieces, proj, low, owned, rank):
    rows, width = inputs.shape[0], pieces[0].shape[1]
    tile = tile_of(width)
    down_rows = owned * rank
    total = len(pieces)
    share = pieces[0].shape[0] - down_rows
    merged = one_sided(count, step) and total > 1
    shared = share * (1 if merged else total)
    held = [] if proj is None else [proj], [] if low is None else [low]

    def body(slot_ref, back_ref, in_ref, *refs):
        place = lax.axis_index("dp")
        blocks = [arrived(count, place, step, odd) if step else place for odd in range(total)]
        slots, ins = slot_ref[...], in_ref[...]
        piece_refs, share_refs, refs = refs[:total], refs[total : 2 * total], refs[2 * total :]
        held_refs, (proj_ref, low_ref, share_ref, factor_ref) = refs[:-4], refs[-4:]

        @pl.when(pl.program_id(0) == 0)
        def prepare():
            for at, block in enumerate(blocks):
                factor_ref[at] = spread(slots, block, back_ref[...], owned, rank)

        if merged:
            came = within(count, blocks[0])
            share_ref[...] = jnp.where(came, share_refs[0][...], share_refs[1][...])
        else:
            for at, ref in enumerate(share_refs):
                share_ref[at * share : (at + 1) * share, :] = ref[...]
        sums, lows = None, None
        for at, block in enumerate(blocks):
            value = piece_refs[at][...]
            term = pick(slots, block, dot(value, ins, 1, 1), owned, rank)
            sums = term if sums is None else sums + term
            term = narrow(dot(factor_ref[at], value, 0, 0))
            lows = term if lows is None else lows + term
        low_ref[...] = lows + held_refs[-1][...] if held[1] else lows

        @pl.when(pl.program_id(0) == 0)
        def first():
            proj_ref[...] = sums + held_refs[0][...] if held[0] else sums

        @pl.when(pl.program_id(0) > 0)
        def later():
            proj_ref[...] = proj_ref[...] + sums

    return call(
        body,
        (width // tile,),
        [full(slot.shape), full(back.shape), columns(rows, tile, stream * (width // tile))]
        + [columns(down_rows, tile)] * total
        + [columns(share, tile, 0, down_rows // share)] * total
        + [full((rank, rows))] * len(held[0])
        + [columns(rows, tile)] * len(held[1]),
        [full((rank, rows)), columns(rows, tile), columns(shared, tile)],
        [
            jax.ShapeDtypeStruct((rank, rows), jnp.float32),
            jax.ShapeDtypeStruct((rows, width), jnp.bfloat16),
            jax.ShapeDtypeStruct((shared, width), jnp.bfloat16),
        ],
        slot,
        back,
        inputs,
        *pieces,
        *pieces,
        *held[0],
        *held[1],
        scratch=[pltpu.VMEM((total, down_rows, rows), jnp.bfloat16)],
        flops=piece_flops if step else 1,
    )


def up_parts(targets, slot, proj, cotangent, owned, rank):
    keys = cotangent.shape[1]

    def body(slot_ref, proj_ref, cot_ref, *outs):
        place = lax.axis_index("dp")
        slots, projs, cots = slot_ref[...], proj_ref[...], cot_ref[...]
        for target, out in zip(targets, outs):
            out[...] = narrow(dot(spread(slots, target(place), projs, owned, rank), cots, 1, 0))

    shape = (owned * rank, keys)
    return call(
        body,
        (1,),
        [full(slot.shape), full(proj.shape), full(cotangent.shape)],
        [full(shape)] * len(targets),
        [jax.ShapeDtypeStruct(shape, jnp.bfloat16)] * len(targets),
        slot,
        proj,
        cotangent,
    )


def pack(down_own, weight):
    down_rows, width = down_own.shape
    keys = weight.shape[1]
    half = weight.shape[0] // lax.axis_size("groups")
    streams = width // keys
    chunk = half // streams

    def body(down_ref, weight_ref, *outs):
        group = lax.axis_index("groups")
        for at, out in enumerate(outs):
            rows = pl.ds(pl.multiple_of(group * half + at * chunk, chunk), chunk)
            out[:down_rows, :] = down_ref[:, at * keys : (at + 1) * keys]
            out[down_rows:, :] = weight_ref[rows, :]

    shape = (down_rows + chunk, keys)
    return call(
        body,
        (1,),
        [full(down_own.shape), full(weight.shape)],
        [full(shape)] * streams,
        [jax.ShapeDtypeStruct(shape, jnp.bfloat16)] * streams,
        down_own,
        weight,
    )


def finish(cotangents, weight_own, described, pieces, lows):
    rows, stream_width = lows[0].shape
    streams = len(lows)
    weight_rows, keys = weight_own.shape
    shard = cotangents[0].shape[1]
    count, groups, parts = lax.axis_size("dp"), lax.axis_size("groups"), len(cotangents)
    half = weight_rows // groups
    chunk = half // streams
    some = max(1, 512 // weight_rows)
    tile = some * weight_rows
    tiles = stream_width // tile

    def body(*refs):
        cot_refs, own_ref, refs = refs[:parts], refs[parts], refs[parts + 1 :]
        piece_refs, low_refs = refs[: len(pieces)], refs[len(pieces) : -3]
        out_ref, dy_ref, weight_ref = refs[-3:]
        now = pl.program_id(0)

        @pl.when(now == 0)
        def arrange():
            place, group, part = (lax.axis_index(axis) for axis in ("dp", "groups", "fsdp"))
            for turn, ref in enumerate(cot_refs):
                at = lax.rem(part + parts - turn, parts) * shard
                dy_ref[:, pl.ds(pl.multiple_of(at, shard), shard)] = ref[...]
            weight_ref[place] = own_ref[...]
            for at, ref in enumerate(piece_refs):
                owner = lax.rem(group + groups - at % groups, groups)
                for first, (step, stream, odds) in enumerate(described[at // groups]):
                    for odd in odds:
                        block = arrived(count, place, step, odd)

                        def store(first=first * chunk, stream=stream, block=block):
                            row = pl.multiple_of(owner * half + stream * chunk, chunk)
                            weight_ref[block, pl.ds(row, chunk), :] = ref[first : first + chunk, :]

                        pl.when(within(count, block))(store)

        def add(low_ref):
            for block in range(some):
                at = slice(block * weight_rows, (block + 1) * weight_rows)
                base = dot(dy_ref[...], weight_ref[now * some + block], 1, 1)
                out_ref[:, at] = narrow(base + low_ref[:, at].astype(jnp.float32))

        for stream, low_ref in enumerate(low_refs):
            pl.when(now // tiles == stream)(functools.partial(add, low_ref))

    def low_spec(stream):
        return pl.BlockSpec((rows, tile), lambda at: (0, jnp.clip(at - stream * tiles, 0, tiles - 1)))

    fixed = [*cotangents, weight_own, *pieces]
    return call(
        body,
        (streams * tiles,),
        [full(array.shape) for array in fixed] + [low_spec(stream) for stream in range(streams)],
        columns(rows, tile),
        jax.ShapeDtypeStruct((rows, streams * stream_width), jnp.bfloat16),
        *fixed,
        *lows,
        scratch=[
            pltpu.VMEM((rows, keys), jnp.bfloat16),
            pltpu.VMEM((count, weight_rows, keys), jnp.bfloat16),
        ],
    )


def shards(
    inputs,
    cotangent,
    frozen_key_weight,
    adapter_down_weight,
    adapter_up_weight,
    row_adapter_index,
    adapter_slot_index,
):
    tok_rows, feat_width = inputs.shape
    key_shard = cotangent.shape[1]
    owned, rank, _ = adapter_down_weight.shape
    slots = adapter_slot_index.shape[0]
    data_count, place = lax.axis_size("dp"), lax.axis_index("dp")
    down_rows = owned * rank
    key_at = lax.axis_index("fsdp") * key_shard

    up_own = lax.dynamic_slice_in_dim(adapter_up_weight, key_at, key_shard, 2)
    up_own = up_own.reshape(down_rows, key_shard)
    ups = [up_own] + turns(up_own, "dp")
    down_own = adapter_down_weight.reshape(down_rows, feat_width)
    packed = pack(down_own, frozen_key_weight)

    ids = row_adapter_index[:, 0]
    every = lax.broadcasted_iota(jnp.int32, (slots, tok_rows), 0)
    slot = jnp.sum(jnp.where(ids[None, :] == every, adapter_slot_index[:, None], 0), axis=0)
    slot = slot[None, :]

    def up_swaps(proj):
        targets, routes = [lambda place: place], []
        for step in range(1, data_count):
            for odd in (0, 1):
                ends = [i for i in range(data_count - step) if i // step % 2 == odd]
                if ends:
                    swaps = [(i, i + step) for i in ends] + [(i + step, i) for i in ends]
                    routes.append(swaps)
                    targets.append(
                        lambda place, step=step, odd=odd: jnp.where(
                            lax.rem(lax.div(place, step), 2) == odd, place + step, place - step
                        )
                    )
        parts = up_parts(targets, slot, proj, cotangent, owned, rank)
        got = [lax.ppermute(part, "dp", swaps) for part, swaps in zip(parts[1:], routes)]
        return [parts[0]] + got

    streams = range(len(packed))
    received = [[one, one] for one in after(packed, ups)]
    got, lows = [[one] for one in packed], [None for _ in streams]
    proj, back, exchanged = None, None, []
    cotangents = [cotangent] + turns(after(cotangent, ups), "fsdp")
    last = [cotangents]
    waited = {step: [] for step in range(data_count + 3)}
    for step in range(1, data_count + 1):
        if step == 2:
            back = back_sum(slot, cotangent, after(ups, received[0], last), owned, rank)
            back = scaled_sum(back, "fsdp")
        for stream in streams:
            sent = []
            for odd, other in enumerate(reversed(received[stream])):
                if step > 1:
                    other = after(other, last, waited[step] if stream == streams[-1] else [])
                if not only_blocks(step, odd):
                    other = message(
                        step, data_count, odd, stream, slot, back, inputs, other, owned, rank
                    )
                sent.append(other)
            received[stream] = [
                lax.ppermute(sent[odd], "dp", pairs(data_count, odd)) for odd in (0, 1)
            ]
            if step == 1:
                continue
            pieces = after(got[stream], sent)
            if step == 2:
                proj, lows[stream], _ = use_pieces(
                    0, data_count, stream, slot, back, inputs, [packed[stream]], proj, None,
                    owned, rank,
                )
            proj, lows[stream], share = use_pieces(
                step - 1, data_count, stream, slot, back, inputs, pieces, proj, lows[stream],
                owned, rank,
            )
            last = [proj, lows[stream]]
            share = [share] + turns(share, "groups")
            waited[step + 1].append(share)
            if one_sided(data_count, step - 1):
                described = [(step - 1, stream, odds)]
            else:
                described = [(step - 1, stream, [odd]) for odd in odds]
            exchanged.append((described, share))
        odds = [odd for odd in (0, 1) if not only_sums(data_count, step, odd)]
        got = [[received[stream][odd] for odd in odds] for stream in streams]

    order = [entry for entry, _ in exchanged]
    parts = sum([share for _, share in exchanged], [])
    input_grad = finish(cotangents, frozen_key_weight, order, parts, lows)
    down_grad = None
    for stream in streams:
        if stream == streams[-1]:
            received[stream] = after(received[stream], input_grad)
        down_grad = own_sum(
            stream, slot, back, inputs, received[stream], down_grad, owned, rank
        )
        if stream == 0:
            proj = scaled_sum(after(proj, down_grad), "fsdp")
            up_grads = up_swaps(proj)
    up_grads = after(up_grads, input_grad)
    up_grad = sum(part.astype(jnp.float32) for part in up_grads)
    return (
        input_grad,
        down_grad.reshape(owned, rank, feat_width),
        narrow(up_grad).reshape(owned, rank, key_shard),
    )


def solution(mesh):
    placed = (
        P(("groups", "dp"), "fsdp"),
        P(("groups", "dp"), "fsdp"),
        P(("fsdp", "dp"), None),
        P(("groups", "dp"), None, "fsdp"),
        P(("groups", "dp"), None, None),
        P(("groups", "dp"), None),
        P("groups"),
    )
    return jax.shard_map(
        shards,
        mesh=mesh,
        in_specs=placed,
        out_specs=(
            P(("groups", "dp"), "fsdp"),
            P(("groups", "dp"), None, "fsdp"),
            P(("groups", "dp"), None, "fsdp"),
        ),
        check_vma=False,
    )
```

```python
import functools

import jax
import jax.numpy as jnp
from jax import lax
from jax.experimental import pallas as pl
from jax.experimental.pallas import tpu as pltpu
from jax.sharding import PartitionSpec as P

adapter_scale = 2.0
piece_flops = 1
vmem_bytes = 24 * 1024 * 1024


def dot(a, b, ca, cb):
    return lax.dot_general(a, b, (((ca,), (cb,)), ((), ())), preferred_element_type=jnp.float32)


def narrow(values):
    return values.astype(jnp.bfloat16)


def turns(value, axis):
    count = lax.axis_size(axis)
    return [
        lax.ppermute(value, axis, [(i, (i + step) % count) for i in range(count)])
        for step in range(1, count)
    ]


def after(value, *others):
    return lax.optimization_barrier((value, others))[0]


def halving(value, axis):
    count = lax.axis_size(axis)
    if count & (count - 1):
        return [value] + turns(value, axis)
    step = 1
    while True:
        other = lax.ppermute(value, axis, [(i, i ^ step) for i in range(count)])
        step *= 2
        if step >= count:
            return [value, other]
        value = value + other


def after(value, *others):
    return lax.optimization_barrier((value, others))[0]


def line_pass(below, above, axis, step):
    count = lax.axis_size(axis)
    up = [(i, i + 1) for i in range(step - 1, count - 1)]
    down = [(i + 1, i) for i in range(count - step)]
    return lax.ppermute(below, axis, up), lax.ppermute(above, axis, down)


def pairs(count, odd):
    swaps = [(i, i + 1) for i in range(odd, count - 1, 2)]
    return swaps + [(b, a) for a, b in swaps]


def going_up(place, odd):
    return lax.rem(place, 2) == odd


def arrived(count, place, step, odd):
    return jnp.where(going_up(place, odd), place + step, place - step)


def within(count, block):
    return (block >= 0) & (block < count)


def one_sided(count, step):
    return 2 * step >= count


def only_sums(count, step, odd):
    return step >= count - odd


def only_blocks(step, odd):
    return step <= 1 + odd


def named(slot, block, owned, rank):
    shape = (owned * rank, slot.shape[1])
    return (slot - block * owned) == lax.broadcasted_iota(jnp.int32, shape, 0) // rank


def pick(slot, block, values, owned, rank):
    values = jnp.where(named(slot, block, owned, rank), values, 0.0)
    total = values[:rank]
    for at in range(1, owned):
        total = total + values[at * rank : (at + 1) * rank]
    return total


def spread(slot, block, values, owned, rank):
    values = jnp.concatenate([values.astype(jnp.float32)] * owned, axis=0)
    return narrow(jnp.where(named(slot, block, owned, rank), values, 0.0))


def columns(height, tile, at_tile=0, at_row=0):
    return pl.BlockSpec((height, tile), lambda at: (at_row, at_tile + at))


def tile_of(width):
    return 512 if width % 512 == 0 else width


def full(shape):
    return pl.BlockSpec(shape, lambda *at: (0,) * len(shape))


def call(body, grid, in_specs, out_specs, out_shape, *operands, scratch=(), aliases=None, flops=1):
    return pl.pallas_call(
        body,
        grid=grid,
        in_specs=in_specs,
        out_specs=out_specs,
        out_shape=out_shape,
        scratch_shapes=scratch,
        input_output_aliases=aliases or {},
        compiler_params=pltpu.CompilerParams(vmem_limit_bytes=vmem_bytes),
        cost_estimate=pl.CostEstimate(flops=flops, bytes_accessed=1, transcendentals=0),
    )(*operands)


def back_sum(slot, cotangent, parts, owned, rank):
    count, rows = len(parts), slot.shape[1]

    def body(slot_ref, cot_ref, *refs):
        place = lax.axis_index("dp")
        slots, cots = slot_ref[...], cot_ref[...]
        total = jnp.zeros((rank, rows), jnp.float32)
        for turn in range(count):
            block = lax.rem(place + count - turn, count)
            total = total + pick(slots, block, dot(refs[turn][...], cots, 1, 1), owned, rank)
        refs[count][...] = total

    return call(
        body,
        (1,),
        [full(slot.shape), full(cotangent.shape)] + [full(part.shape) for part in parts],
        full((rank, rows)),
        jax.ShapeDtypeStruct((rank, rows), jnp.float32),
        slot,
        cotangent,
        *parts,
    )


def add_up(parts, last):
    def body(*refs):
        total = refs[0][...]
        for ref in refs[1:-1]:
            total = total + ref[...]
        if last:
            total = narrow(adapter_scale * narrow(total).astype(jnp.float32))
        refs[-1][...] = total

    shape = parts[0].shape
    return call(
        body,
        (1,),
        [full(shape)] * len(parts),
        full(shape),
        jax.ShapeDtypeStruct(shape, jnp.bfloat16 if last else jnp.float32),
        *parts,
    )


def scaled_sum(value, axis):
    count = lax.axis_size(axis)
    if count & (count - 1):
        return add_up([value] + turns(value, axis), True)
    step = 1
    while step < count:
        other = lax.ppermute(value, axis, [(i, i ^ step) for i in range(count)])
        step *= 2
        value = add_up([value, other], step >= count)
    return value


def message(step, count, odd, stream, slot, back, inputs, received, extra, owned, rank):
    rows, width = inputs.shape[0], received.shape[1]
    tile = tile_of(width)
    down_rows = owned * rank
    height = down_rows if only_sums(count, step, odd) else received.shape[0]
    given, below, across = [], 0, 1
    if extra is not None:
        given, across = [extra], tile // extra.shape[1]
        below = down_rows * extra.shape[1] // width

    def body(slot_ref, back_ref, in_ref, got_ref, *refs):
        out_ref, factor_ref = refs[-2:]
        place = lax.axis_index("dp")
        up = going_up(place, odd)
        along = jnp.where(up, place, count - 1 - place)
        target = along + count - step + 1
        block = jnp.where(up, target, count - 1 - target)

        @pl.when(pl.program_id(0) == 0)
        def prepare():
            factor_ref[...] = spread(slot_ref[...], block, back_ref[...], owned, rank)

        def add():
            value = dot(factor_ref[...], in_ref[...], 1, 0)
            out_ref[:down_rows, :] = narrow(value + got_ref[:down_rows, :].astype(jnp.float32))
            for at in range(across if given else 0):
                lanes = slice(at * extra.shape[1], (at + 1) * extra.shape[1])
                out_ref[down_rows:, lanes] = refs[0][at * below : (at + 1) * below, :]
            if height > down_rows:
                out_ref[down_rows:, :] = jnp.zeros((height - down_rows, tile), jnp.bfloat16)

        def pass_on():
            out_ref[...] = got_ref[...]

        if height == down_rows:
            add()
        else:
            pl.when(along < step - 1)(add)
            pl.when(along >= step - 1)(pass_on)

    return call(
        body,
        (width // tile,),
        [
            full(slot.shape),
            full(back.shape),
            columns(rows, tile, stream * (width // tile)),
            columns(height, tile),
        ]
        + [pl.BlockSpec((below * across, one.shape[1]), lambda at: (at, 0)) for one in given],
        columns(height + below, tile),
        jax.ShapeDtypeStruct((height + below, width), jnp.bfloat16),
        slot,
        back,
        inputs,
        received,
        *given,
        scratch=[pltpu.VMEM((down_rows, rows), jnp.bfloat16)],
    )


def own_sum(stream, slot, back, inputs, received, whole, owned, rank):
    rows, width = inputs.shape[0], received[0].shape[1]
    tile = tile_of(width)
    down_rows = owned * rank
    first = stream * (width // tile)
    given = [] if whole is None else [whole]

    def body(slot_ref, back_ref, in_ref, *refs):
        out_ref, factor_ref = refs[-2:]

        @pl.when(pl.program_id(0) == 0)
        def prepare():
            place = lax.axis_index("dp")
            factor_ref[...] = spread(slot_ref[...], place, back_ref[...], owned, rank)

        value = dot(factor_ref[...], in_ref[...], 1, 0)
        for ref in refs[: len(received)]:
            value = value + ref[...].astype(jnp.float32)
        out_ref[...] = narrow(value)

    return call(
        body,
        (width // tile,),
        [full(slot.shape), full(back.shape), columns(rows, tile, first)]
        + [columns(down_rows, tile)] * len(received)
        + [pl.BlockSpec(memory_space=pl.ANY)] * len(given),
        columns(down_rows, tile, first),
        jax.ShapeDtypeStruct((down_rows, inputs.shape[1]), jnp.bfloat16),
        slot,
        back,
        inputs,
        *received,
        *given,
        scratch=[pltpu.VMEM((down_rows, rows), jnp.bfloat16)],
        aliases={3 + len(received): 0} if given else None,
    )


def use_pieces(step, count, stream, slot, back, inputs, pieces, proj, low, prior, owned, rank):
    rows, width = inputs.shape[0], pieces[0].shape[1]
    tile = tile_of(width)
    down_rows = owned * rank
    total = len(pieces)
    share = pieces[0].shape[0] - down_rows
    merged = one_sided(count, step) and total > 1
    shared = share * (1 if merged else total)
    held = [] if proj is None else [proj], [] if low is None else [low]
    given = [] if prior is None else [prior]
    above = 0 if prior is None else prior.shape[0]

    def body(slot_ref, back_ref, in_ref, *refs):
        place = lax.axis_index("dp")
        blocks = [arrived(count, place, step, odd) if step else place for odd in range(total)]
        slots, ins = slot_ref[...], in_ref[...]
        piece_refs, share_refs, refs = refs[:total], refs[total : 2 * total], refs[2 * total :]
        held_refs, (proj_ref, low_ref, share_ref, factor_ref) = refs[:-4], refs[-4:]
        if given:
            share_ref[:above, :] = held_refs[-1][...]
            held_refs = held_refs[:-1]

        @pl.when(pl.program_id(0) == 0)
        def prepare():
            for at, block in enumerate(blocks):
                factor_ref[at] = spread(slots, block, back_ref[...], owned, rank)

        if merged:
            came = within(count, blocks[0])
            share_ref[above:, :] = jnp.where(came, share_refs[0][...], share_refs[1][...])
        else:
            for at, ref in enumerate(share_refs):
                share_ref[above + at * share : above + (at + 1) * share, :] = ref[...]
        sums, lows = None, None
        for at, block in enumerate(blocks):
            value = piece_refs[at][...]
            term = pick(slots, block, dot(value, ins, 1, 1), owned, rank)
            sums = term if sums is None else sums + term
            term = narrow(dot(factor_ref[at], value, 0, 0))
            lows = term if lows is None else lows + term
        low_ref[...] = lows + held_refs[-1][...] if held[1] else lows

        @pl.when(pl.program_id(0) == 0)
        def first():
            proj_ref[...] = sums + held_refs[0][...] if held[0] else sums

        @pl.when(pl.program_id(0) > 0)
        def later():
            proj_ref[...] = proj_ref[...] + sums

    return call(
        body,
        (width // tile,),
        [full(slot.shape), full(back.shape), columns(rows, tile, stream * (width // tile))]
        + [columns(down_rows, tile)] * total
        + [columns(share, tile, 0, down_rows // share)] * total
        + [full((rank, rows))] * len(held[0])
        + [columns(rows, tile)] * len(held[1])
        + [columns(above, tile)] * len(given),
        [full((rank, rows)), columns(rows, tile), columns(above + shared, tile)],
        [
            jax.ShapeDtypeStruct((rank, rows), jnp.float32),
            jax.ShapeDtypeStruct((rows, width), jnp.bfloat16),
            jax.ShapeDtypeStruct((above + shared, width), jnp.bfloat16),
        ],
        slot,
        back,
        inputs,
        *pieces,
        *pieces,
        *held[0],
        *held[1],
        *given,
        scratch=[pltpu.VMEM((total, down_rows, rows), jnp.bfloat16)],
        flops=piece_flops if step else 1,
    )


def up_parts(targets, slot, proj, cotangent, owned, rank):
    keys = cotangent.shape[1]

    def body(slot_ref, proj_ref, cot_ref, *outs):
        place = lax.axis_index("dp")
        slots, projs, cots = slot_ref[...], proj_ref[...], cot_ref[...]
        for target, out in zip(targets, outs):
            out[...] = narrow(dot(spread(slots, target(place), projs, owned, rank), cots, 1, 0))

    shape = (owned * rank, keys)
    return call(
        body,
        (1,),
        [full(slot.shape), full(proj.shape), full(cotangent.shape)],
        [full(shape)] * len(targets),
        [jax.ShapeDtypeStruct(shape, jnp.bfloat16)] * len(targets),
        slot,
        proj,
        cotangent,
    )


def up_total(own, swapped, others):
    height, keys = own.shape
    width = swapped[0].shape[1]
    across = width // keys
    below = height // across

    def body(*refs):
        own_ref, swapped_refs, other_refs = refs[0], refs[1 : 1 + len(swapped)], refs[1 + len(swapped) : -1]
        for at in range(across):
            rows, lanes = slice(at * below, (at + 1) * below), slice(at * keys, (at + 1) * keys)
            total = own_ref[rows, :].astype(jnp.float32)
            for ref in swapped_refs:
                total = total + ref[:, lanes].astype(jnp.float32)
            for ref in other_refs:
                total = total + ref[rows, :].astype(jnp.float32)
            refs[-1][rows, :] = narrow(total)

    return call(
        body,
        (1,),
        [full(own.shape)]
        + [pl.BlockSpec((below, width), lambda at: (height // below, 0))] * len(swapped)
        + [full(own.shape)] * len(others),
        full(own.shape),
        jax.ShapeDtypeStruct(own.shape, jnp.bfloat16),
        own,
        *swapped,
        *others,
    )


def pack(down_own, weight):
    down_rows, width = down_own.shape
    keys = weight.shape[1]
    half = weight.shape[0] // lax.axis_size("groups")
    streams = width // keys
    chunk = half // streams

    def body(down_ref, weight_ref, *outs):
        group = lax.axis_index("groups")
        for at, out in enumerate(outs):
            rows = pl.ds(pl.multiple_of(group * half + at * chunk, chunk), chunk)
            out[:down_rows, :] = down_ref[:, at * keys : (at + 1) * keys]
            out[down_rows:, :] = weight_ref[rows, :]

    shape = (down_rows + chunk, keys)
    return call(
        body,
        (1,),
        [full(down_own.shape), full(weight.shape)],
        [full(shape)] * streams,
        [jax.ShapeDtypeStruct(shape, jnp.bfloat16)] * streams,
        down_own,
        weight,
    )


def finish(cotangents, weight_own, described, pieces, lows):
    rows, stream_width = lows[0].shape
    streams = len(lows)
    weight_rows, keys = weight_own.shape
    shard = cotangents[0].shape[1]
    count, groups, parts = lax.axis_size("dp"), lax.axis_size("groups"), len(cotangents)
    half = weight_rows // groups
    chunk = half // streams
    some = max(1, 512 // weight_rows)
    tile = some * weight_rows
    tiles = stream_width // tile

    def body(*refs):
        cot_refs, own_ref, refs = refs[:parts], refs[parts], refs[parts + 1 :]
        piece_refs, low_refs = refs[: len(pieces)], refs[len(pieces) : -3]
        out_ref, dy_ref, weight_ref = refs[-3:]
        now = pl.program_id(0)

        @pl.when(now == 0)
        def arrange():
            place, group, part = (lax.axis_index(axis) for axis in ("dp", "groups", "fsdp"))
            for turn, ref in enumerate(cot_refs):
                at = lax.rem(part + parts - turn, parts) * shard
                dy_ref[:, pl.ds(pl.multiple_of(at, shard), shard)] = ref[...]
            weight_ref[place] = own_ref[...]
            for at, ref in enumerate(piece_refs):
                owner = lax.rem(group + groups - at % groups, groups)
                for first, (step, stream, odds) in enumerate(described[at // groups]):
                    for odd in odds:
                        block = arrived(count, place, step, odd)

                        def store(first=first * chunk, stream=stream, block=block):
                            row = pl.multiple_of(owner * half + stream * chunk, chunk)
                            weight_ref[block, pl.ds(row, chunk), :] = ref[first : first + chunk, :]

                        pl.when(within(count, block))(store)

        def add(low_ref):
            for block in range(some):
                at = slice(block * weight_rows, (block + 1) * weight_rows)
                base = dot(dy_ref[...], weight_ref[now * some + block], 1, 1)
                out_ref[:, at] = narrow(base + low_ref[:, at].astype(jnp.float32))

        for stream, low_ref in enumerate(low_refs):
            pl.when(now // tiles == stream)(functools.partial(add, low_ref))

    def low_spec(stream):
        return pl.BlockSpec((rows, tile), lambda at: (0, jnp.clip(at - stream * tiles, 0, tiles - 1)))

    fixed = [*cotangents, weight_own, *pieces]
    return call(
        body,
        (streams * tiles,),
        [full(array.shape) for array in fixed] + [low_spec(stream) for stream in range(streams)],
        columns(rows, tile),
        jax.ShapeDtypeStruct((rows, streams * stream_width), jnp.bfloat16),
        *fixed,
        *lows,
        scratch=[
            pltpu.VMEM((rows, keys), jnp.bfloat16),
            pltpu.VMEM((count, weight_rows, keys), jnp.bfloat16),
        ],
    )


def shards(
    inputs,
    cotangent,
    frozen_key_weight,
    adapter_down_weight,
    adapter_up_weight,
    row_adapter_index,
    adapter_slot_index,
):
    tok_rows, feat_width = inputs.shape
    key_shard = cotangent.shape[1]
    owned, rank, _ = adapter_down_weight.shape
    slots = adapter_slot_index.shape[0]
    data_count, place = lax.axis_size("dp"), lax.axis_index("dp")
    down_rows = owned * rank
    key_at = lax.axis_index("fsdp") * key_shard

    up_own = lax.dynamic_slice_in_dim(adapter_up_weight, key_at, key_shard, 2)
    up_own = up_own.reshape(down_rows, key_shard)
    ups = [up_own] + turns(up_own, "dp")
    down_own = adapter_down_weight.reshape(down_rows, feat_width)
    packed = pack(down_own, frozen_key_weight)

    ids = row_adapter_index[:, 0]
    every = lax.broadcasted_iota(jnp.int32, (slots, tok_rows), 0)
    slot = jnp.sum(jnp.where(ids[None, :] == every, adapter_slot_index[:, None], 0), axis=0)
    slot = slot[None, :]

    def up_ways(step):
        ways = []
        for odd in (0, 1):
            ends = [i for i in range(data_count - step) if i // step % 2 == odd]

            def other(place, odd=odd):
                mine = lax.rem(lax.div(place, step), 2) == odd
                return jnp.where(mine, place + step, place - step)

            if ends:
                swaps = [(i, i + step) for i in ends] + [(i + step, i) for i in ends]
                ways.append((other, swaps))
        return ways

    def own_block(place):
        return place

    streams = range(len(packed))
    received = [[one, one] for one in after(packed, ups)]
    got, lows = [[one] for one in packed], [None for _ in streams]
    proj, back, exchanged, extras = None, None, [], [None, None]
    cotangents = [cotangent] + turns(after(cotangent, ups), "fsdp")
    last = [cotangents]
    waited = {step: [] for step in range(data_count + 3)}
    for step in range(1, data_count + 1):
        if step == 2:
            back = back_sum(slot, cotangent, after(ups, received[0], last), owned, rank)
            back = scaled_sum(back, "fsdp")
        for stream in streams:
            sent = []
            for odd, other in enumerate(reversed(received[stream])):
                if step > 1:
                    other = after(other, last, waited[step] if stream == streams[-1] else [])
                if not only_blocks(step, odd):
                    extra = extras[odd] if stream == streams[-1] else None
                    other = message(
                        step, data_count, odd, stream, slot, back, inputs, other, extra, owned, rank
                    )
                sent.append(other)
            received[stream] = [
                lax.ppermute(sent[odd], "dp", pairs(data_count, odd)) for odd in (0, 1)
            ]
            if step == 1:
                continue
            pieces = after(got[stream], sent)
            if step == 2:
                proj, lows[stream], _ = use_pieces(
                    0, data_count, stream, slot, back, inputs, [packed[stream]], proj, None,
                    None, owned, rank,
                )
            merged = one_sided(data_count, step - 1)
            if stream == 0 or not merged:
                prior, described = None, []
            proj, lows[stream], share = use_pieces(
                step - 1, data_count, stream, slot, back, inputs, pieces, proj, lows[stream],
                prior, owned, rank,
            )
            last = [proj, lows[stream]]
            described += [(step - 1, stream, some) for some in ([odds] if merged else [[odd] for odd in odds])]
            prior = share
            if stream == streams[-1] or not merged:
                share = [share] + turns(share, "groups")
                waited[step + 1].append(share)
                exchanged.append((described, share))
        if step == data_count - 1:
            near = scaled_sum(proj, "fsdp")
            ways = sum([up_ways(away) for away in range(1, step)], [])
            targets = [own_block] + [other for other, _ in ways]
            up_own, *parts = up_parts(targets, slot, near, cotangent, owned, rank)
            extras = parts[:2]
            waiting = [(part, way) for part, (_, way) in zip(parts[2:], ways[2:])]
            proj = None
        odds = [odd for odd in (0, 1) if not only_sums(data_count, step, odd)]
        got = [[received[stream][odd] for odd in odds] for stream in streams]

    order = [entry for entry, _ in exchanged]
    parts = sum([share for _, share in exchanged], [])
    input_grad = finish(cotangents, frozen_key_weight, order, parts, lows)
    down_grad = None
    for stream in streams:
        if stream == streams[-1]:
            received[stream] = after(received[stream], input_grad)
        down_grad = own_sum(
            stream, slot, back, inputs, received[stream], down_grad, owned, rank
        )
        if stream == 0:
            others = [lax.ppermute(after(part, down_grad), "dp", way) for part, way in waiting]
            far = scaled_sum(after(proj, down_grad), "fsdp")
            ways = up_ways(data_count - 1)
            parts = up_parts([other for other, _ in ways], slot, far, cotangent, owned, rank)
            others += [lax.ppermute(part, "dp", way) for part, (_, way) in zip(parts, ways)]
    others = after(others, input_grad)
    up_grad = up_total(up_own, received[streams[-1]], others)
    return (
        input_grad,
        down_grad.reshape(owned, rank, feat_width),
        up_grad.reshape(owned, rank, key_shard),
    )


def solution(mesh):
    placed = (
        P(("groups", "dp"), "fsdp"),
        P(("groups", "dp"), "fsdp"),
        P(("fsdp", "dp"), None),
        P(("groups", "dp"), None, "fsdp"),
        P(("groups", "dp"), None, None),
        P(("groups", "dp"), None),
        P("groups"),
    )
    return jax.shard_map(
        shards,
        mesh=mesh,
        in_specs=placed,
        out_specs=(
            P(("groups", "dp"), "fsdp"),
            P(("groups", "dp"), None, "fsdp"),
            P(("groups", "dp"), None, "fsdp"),
        ),
        check_vma=False,
    )
```

```python
import functools

import jax
import jax.numpy as jnp
from jax import lax
from jax.experimental import pallas as pl
from jax.experimental.pallas import tpu as pltpu
from jax.sharding import PartitionSpec as P

adapter_scale = 2.0
piece_flops = 1
back_flops = 10**10
vmem_bytes = 24 * 1024 * 1024


def dot(a, b, ca, cb):
    return lax.dot_general(a, b, (((ca,), (cb,)), ((), ())), preferred_element_type=jnp.float32)


def narrow(values):
    return values.astype(jnp.bfloat16)


def turns(value, axis):
    count = lax.axis_size(axis)
    return [
        lax.ppermute(value, axis, [(i, (i + step) % count) for i in range(count)])
        for step in range(1, count)
    ]


def after(value, *others):
    return lax.optimization_barrier((value, others))[0]


def halving(value, axis):
    count = lax.axis_size(axis)
    if count & (count - 1):
        return [value] + turns(value, axis)
    step = 1
    while True:
        other = lax.ppermute(value, axis, [(i, i ^ step) for i in range(count)])
        step *= 2
        if step >= count:
            return [value, other]
        value = value + other


def after(value, *others):
    return lax.optimization_barrier((value, others))[0]


def line_pass(below, above, axis, step):
    count = lax.axis_size(axis)
    up = [(i, i + 1) for i in range(step - 1, count - 1)]
    down = [(i + 1, i) for i in range(count - step)]
    return lax.ppermute(below, axis, up), lax.ppermute(above, axis, down)


def pairs(count, odd):
    swaps = [(i, i + 1) for i in range(odd, count - 1, 2)]
    return swaps + [(b, a) for a, b in swaps]


def going_up(place, odd):
    return lax.rem(place, 2) == odd


def arrived(count, place, step, odd):
    return jnp.where(going_up(place, odd), place + step, place - step)


def within(count, block):
    return (block >= 0) & (block < count)


def one_sided(count, step):
    return 2 * step >= count


def only_sums(count, step, odd):
    return step >= count - odd


def only_blocks(step, odd):
    return step <= 1 + odd


def named(slot, block, owned, rank):
    shape = (owned * rank, slot.shape[1])
    return (slot - block * owned) == lax.broadcasted_iota(jnp.int32, shape, 0) // rank


def pick(slot, block, values, owned, rank):
    values = jnp.where(named(slot, block, owned, rank), values, 0.0)
    total = values[:rank]
    for at in range(1, owned):
        total = total + values[at * rank : (at + 1) * rank]
    return total


def spread(slot, block, values, owned, rank):
    values = jnp.concatenate([values.astype(jnp.float32)] * owned, axis=0)
    return narrow(jnp.where(named(slot, block, owned, rank), values, 0.0))


def columns(height, tile, at_tile=0, at_row=0):
    return pl.BlockSpec((height, tile), lambda at: (at_row, at_tile + at))


def tile_of(width):
    return 512 if width % 512 == 0 else width


def full(shape):
    return pl.BlockSpec(shape, lambda *at: (0,) * len(shape))


def call(body, grid, in_specs, out_specs, out_shape, *operands, scratch=(), aliases=None, flops=1):
    return pl.pallas_call(
        body,
        grid=grid,
        in_specs=in_specs,
        out_specs=out_specs,
        out_shape=out_shape,
        scratch_shapes=scratch,
        input_output_aliases=aliases or {},
        compiler_params=pltpu.CompilerParams(vmem_limit_bytes=vmem_bytes),
        cost_estimate=pl.CostEstimate(flops=flops, bytes_accessed=1, transcendentals=0),
    )(*operands)


def back_sum(slot, cotangent, parts, owned, rank):
    count, rows = len(parts), slot.shape[1]

    def body(slot_ref, cot_ref, *refs):
        place = lax.axis_index("dp")
        slots, cots = slot_ref[...], cot_ref[...]
        total = jnp.zeros((rank, rows), jnp.float32)
        for turn in range(count):
            block = lax.rem(place + count - turn, count)
            total = total + pick(slots, block, dot(refs[turn][...], cots, 1, 1), owned, rank)
        refs[count][...] = total

    return call(
        body,
        (1,),
        [full(slot.shape), full(cotangent.shape)] + [full(part.shape) for part in parts],
        full((rank, rows)),
        jax.ShapeDtypeStruct((rank, rows), jnp.float32),
        slot,
        cotangent,
        *parts,
        flops=back_flops,
    )


def add_up(parts, last):
    def body(*refs):
        total = refs[0][...]
        for ref in refs[1:-1]:
            total = total + ref[...]
        if last:
            total = narrow(adapter_scale * narrow(total).astype(jnp.float32))
        refs[-1][...] = total

    shape = parts[0].shape
    return call(
        body,
        (1,),
        [full(shape)] * len(parts),
        full(shape),
        jax.ShapeDtypeStruct(shape, jnp.bfloat16 if last else jnp.float32),
        *parts,
    )


def scaled_sum(value, axis):
    count = lax.axis_size(axis)
    if count & (count - 1):
        return add_up([value] + turns(value, axis), True)
    step = 1
    while step < count:
        other = lax.ppermute(value, axis, [(i, i ^ step) for i in range(count)])
        step *= 2
        value = add_up([value, other], step >= count)
    return value


def stacked(arrays):
    heights = [array.shape[0] for array in arrays]
    shape = (sum(heights), arrays[0].shape[1])

    def body(*refs):
        at = 0
        for ref, height in zip(refs, heights):
            refs[-1][at : at + height, :] = ref[...]
            at += height

    return call(
        body,
        (1,),
        [full(array.shape) for array in arrays],
        full(shape),
        jax.ShapeDtypeStruct(shape, arrays[0].dtype),
        *arrays,
    )


def gathered(value, axis):
    count = lax.axis_size(axis)
    found = [(value, [lambda part: part])]
    if count & (count - 1):
        for turn, other in enumerate(turns(value, axis), 1):
            found.append((other, [lambda part, turn=turn: lax.rem(part + count - turn, count)]))
        return found
    step = 1
    while step < count:
        whole = stacked([array for array, _ in found]) if step > 1 else value
        other = lax.ppermute(whole, axis, [(i, i ^ step) for i in range(count)])
        owners = [
            lambda part, far=step + near: lax.bitwise_xor(part, jnp.int32(far))
            for near in range(step)
        ]
        found.append((other, owners))
        step *= 2
    return found


def message(step, count, odd, stream, slot, back, inputs, received, extra, owned, rank):
    rows, width = inputs.shape[0], received.shape[1]
    tile = tile_of(width)
    down_rows = owned * rank
    height = down_rows if only_sums(count, step, odd) else received.shape[0]
    given, below, across = [], 0, 1
    if extra is not None:
        given, across = [extra], tile // extra.shape[1]
        below = down_rows * extra.shape[1] // width

    def body(slot_ref, back_ref, in_ref, got_ref, *refs):
        out_ref, factor_ref = refs[-2:]
        place = lax.axis_index("dp")
        up = going_up(place, odd)
        along = jnp.where(up, place, count - 1 - place)
        target = along + count - step + 1
        block = jnp.where(up, target, count - 1 - target)

        @pl.when(pl.program_id(0) == 0)
        def prepare():
            factor_ref[...] = spread(slot_ref[...], block, back_ref[...], owned, rank)

        def add():
            value = dot(factor_ref[...], in_ref[...], 1, 0)
            out_ref[:down_rows, :] = narrow(value + got_ref[:down_rows, :].astype(jnp.float32))
            for at in range(across if given else 0):
                lanes = slice(at * extra.shape[1], (at + 1) * extra.shape[1])
                out_ref[down_rows:, lanes] = refs[0][at * below : (at + 1) * below, :]
            if height > down_rows:
                out_ref[down_rows:, :] = jnp.zeros((height - down_rows, tile), jnp.bfloat16)

        def pass_on():
            out_ref[...] = got_ref[...]

        if height == down_rows:
            add()
        else:
            pl.when(along < step - 1)(add)
            pl.when(along >= step - 1)(pass_on)

    return call(
        body,
        (width // tile,),
        [
            full(slot.shape),
            full(back.shape),
            columns(rows, tile, stream * (width // tile)),
            columns(height, tile),
        ]
        + [pl.BlockSpec((below * across, one.shape[1]), lambda at: (at, 0)) for one in given],
        columns(height + below, tile),
        jax.ShapeDtypeStruct((height + below, width), jnp.bfloat16),
        slot,
        back,
        inputs,
        received,
        *given,
        scratch=[pltpu.VMEM((down_rows, rows), jnp.bfloat16)],
    )


def own_sum(stream, slot, back, inputs, received, whole, owned, rank):
    rows, width = inputs.shape[0], received[0].shape[1]
    tile = tile_of(width)
    down_rows = owned * rank
    first = stream * (width // tile)
    given = [] if whole is None else [whole]

    def body(slot_ref, back_ref, in_ref, *refs):
        out_ref, factor_ref = refs[-2:]

        @pl.when(pl.program_id(0) == 0)
        def prepare():
            place = lax.axis_index("dp")
            factor_ref[...] = spread(slot_ref[...], place, back_ref[...], owned, rank)

        value = dot(factor_ref[...], in_ref[...], 1, 0)
        for ref in refs[: len(received)]:
            value = value + ref[...].astype(jnp.float32)
        out_ref[...] = narrow(value)

    return call(
        body,
        (width // tile,),
        [full(slot.shape), full(back.shape), columns(rows, tile, first)]
        + [columns(down_rows, tile)] * len(received)
        + [pl.BlockSpec(memory_space=pl.ANY)] * len(given),
        columns(down_rows, tile, first),
        jax.ShapeDtypeStruct((down_rows, inputs.shape[1]), jnp.bfloat16),
        slot,
        back,
        inputs,
        *received,
        *given,
        scratch=[pltpu.VMEM((down_rows, rows), jnp.bfloat16)],
        aliases={3 + len(received): 0} if given else None,
    )


def use_pieces(step, count, stream, slot, back, inputs, pieces, proj, low, prior, owned, rank):
    rows, width = inputs.shape[0], pieces[0].shape[1]
    tile = tile_of(width)
    down_rows = owned * rank
    total = len(pieces)
    share = pieces[0].shape[0] - down_rows
    merged = one_sided(count, step) and total > 1
    shared = share * (1 if merged else total)
    held = [] if proj is None else [proj], [] if low is None else [low]
    given = [] if prior is None else [prior]
    above = 0 if prior is None else prior.shape[0]

    def body(slot_ref, back_ref, in_ref, *refs):
        place = lax.axis_index("dp")
        blocks = [arrived(count, place, step, odd) if step else place for odd in range(total)]
        slots, ins = slot_ref[...], in_ref[...]
        piece_refs, share_refs, refs = refs[:total], refs[total : 2 * total], refs[2 * total :]
        held_refs, (proj_ref, low_ref, share_ref, factor_ref) = refs[:-4], refs[-4:]
        if given:
            share_ref[:above, :] = held_refs[-1][...]
            held_refs = held_refs[:-1]

        @pl.when(pl.program_id(0) == 0)
        def prepare():
            for at, block in enumerate(blocks):
                factor_ref[at] = spread(slots, block, back_ref[...], owned, rank)

        if merged:
            came = within(count, blocks[0])
            share_ref[above:, :] = jnp.where(came, share_refs[0][...], share_refs[1][...])
        else:
            for at, ref in enumerate(share_refs):
                share_ref[above + at * share : above + (at + 1) * share, :] = ref[...]
        sums, lows = None, None
        for at, block in enumerate(blocks):
            value = piece_refs[at][...]
            term = pick(slots, block, dot(value, ins, 1, 1), owned, rank)
            sums = term if sums is None else sums + term
            term = narrow(dot(factor_ref[at], value, 0, 0))
            lows = term if lows is None else lows + term
        low_ref[...] = lows + held_refs[-1][...] if held[1] else lows

        @pl.when(pl.program_id(0) == 0)
        def first():
            proj_ref[...] = sums + held_refs[0][...] if held[0] else sums

        @pl.when(pl.program_id(0) > 0)
        def later():
            proj_ref[...] = proj_ref[...] + sums

    return call(
        body,
        (width // tile,),
        [full(slot.shape), full(back.shape), columns(rows, tile, stream * (width // tile))]
        + [columns(down_rows, tile)] * total
        + [columns(share, tile, 0, down_rows // share)] * total
        + [full((rank, rows))] * len(held[0])
        + [columns(rows, tile)] * len(held[1])
        + [columns(above, tile)] * len(given),
        [full((rank, rows)), columns(rows, tile), columns(above + shared, tile)],
        [
            jax.ShapeDtypeStruct((rank, rows), jnp.float32),
            jax.ShapeDtypeStruct((rows, width), jnp.bfloat16),
            jax.ShapeDtypeStruct((above + shared, width), jnp.bfloat16),
        ],
        slot,
        back,
        inputs,
        *pieces,
        *pieces,
        *held[0],
        *held[1],
        *given,
        scratch=[pltpu.VMEM((total, down_rows, rows), jnp.bfloat16)],
        flops=piece_flops if step else 1,
    )


def up_parts(targets, slot, proj, cotangent, owned, rank):
    keys = cotangent.shape[1]

    def body(slot_ref, proj_ref, cot_ref, *outs):
        place = lax.axis_index("dp")
        slots, projs, cots = slot_ref[...], proj_ref[...], cot_ref[...]
        for target, out in zip(targets, outs):
            out[...] = narrow(dot(spread(slots, target(place), projs, owned, rank), cots, 1, 0))

    shape = (owned * rank, keys)
    return call(
        body,
        (1,),
        [full(slot.shape), full(proj.shape), full(cotangent.shape)],
        [full(shape)] * len(targets),
        [jax.ShapeDtypeStruct(shape, jnp.bfloat16)] * len(targets),
        slot,
        proj,
        cotangent,
    )


def up_total(own, swapped, others):
    height, keys = own.shape
    width = swapped[0].shape[1]
    across = width // keys
    below = height // across

    def body(*refs):
        own_ref, swapped_refs, other_refs = refs[0], refs[1 : 1 + len(swapped)], refs[1 + len(swapped) : -1]
        for at in range(across):
            rows, lanes = slice(at * below, (at + 1) * below), slice(at * keys, (at + 1) * keys)
            total = own_ref[rows, :].astype(jnp.float32)
            for ref in swapped_refs:
                total = total + ref[:, lanes].astype(jnp.float32)
            for ref in other_refs:
                total = total + ref[rows, :].astype(jnp.float32)
            refs[-1][rows, :] = narrow(total)

    return call(
        body,
        (1,),
        [full(own.shape)]
        + [pl.BlockSpec((below, width), lambda at: (height // below, 0))] * len(swapped)
        + [full(own.shape)] * len(others),
        full(own.shape),
        jax.ShapeDtypeStruct(own.shape, jnp.bfloat16),
        own,
        *swapped,
        *others,
    )


def pack(down_own, weight):
    down_rows, width = down_own.shape
    keys = weight.shape[1]
    half = weight.shape[0] // lax.axis_size("groups")
    streams = width // keys
    chunk = half // streams

    def body(down_ref, weight_ref, *outs):
        group = lax.axis_index("groups")
        for at, out in enumerate(outs):
            rows = pl.ds(pl.multiple_of(group * half + at * chunk, chunk), chunk)
            out[:down_rows, :] = down_ref[:, at * keys : (at + 1) * keys]
            out[down_rows:, :] = weight_ref[rows, :]

    shape = (down_rows + chunk, keys)
    return call(
        body,
        (1,),
        [full(down_own.shape), full(weight.shape)],
        [full(shape)] * streams,
        [jax.ShapeDtypeStruct(shape, jnp.bfloat16)] * streams,
        down_own,
        weight,
    )


def finish(cotangents, weight_own, described, pieces, lows):
    rows, stream_width = lows[0].shape
    streams = len(lows)
    weight_rows, keys = weight_own.shape
    shard = cotangents[0][0].shape[1]
    count, groups, parts = lax.axis_size("dp"), lax.axis_size("groups"), len(cotangents)
    half = weight_rows // groups
    chunk = half // streams
    some = max(1, 512 // weight_rows)
    tile = some * weight_rows
    tiles = stream_width // tile

    def body(*refs):
        cot_refs, own_ref, refs = refs[:parts], refs[parts], refs[parts + 1 :]
        piece_refs, low_refs = refs[: len(pieces)], refs[len(pieces) : -3]
        out_ref, dy_ref, weight_ref = refs[-3:]
        now = pl.program_id(0)

        @pl.when(now == 0)
        def arrange():
            place, group, part = (lax.axis_index(axis) for axis in ("dp", "groups", "fsdp"))
            for ref, (_, owners) in zip(cot_refs, cotangents):
                for at, owner in enumerate(owners):
                    lanes = pl.ds(pl.multiple_of(owner(part) * shard, shard), shard)
                    dy_ref[:, lanes] = ref[at * rows : (at + 1) * rows, :]
            weight_ref[place] = own_ref[...]
            for at, ref in enumerate(piece_refs):
                owner = lax.rem(group + groups - at % groups, groups)
                for first, (step, stream, odds) in enumerate(described[at // groups]):
                    for odd in odds:
                        block = arrived(count, place, step, odd)

                        def store(first=first * chunk, stream=stream, block=block):
                            row = pl.multiple_of(owner * half + stream * chunk, chunk)
                            weight_ref[block, pl.ds(row, chunk), :] = ref[first : first + chunk, :]

                        pl.when(within(count, block))(store)

        def add(low_ref):
            for block in range(some):
                at = slice(block * weight_rows, (block + 1) * weight_rows)
                base = dot(dy_ref[...], weight_ref[now * some + block], 1, 1)
                out_ref[:, at] = narrow(base + low_ref[:, at].astype(jnp.float32))

        for stream, low_ref in enumerate(low_refs):
            pl.when(now // tiles == stream)(functools.partial(add, low_ref))

    def low_spec(stream):
        return pl.BlockSpec((rows, tile), lambda at: (0, jnp.clip(at - stream * tiles, 0, tiles - 1)))

    fixed = [*[array for array, _ in cotangents], weight_own, *pieces]
    return call(
        body,
        (streams * tiles,),
        [full(array.shape) for array in fixed] + [low_spec(stream) for stream in range(streams)],
        columns(rows, tile),
        jax.ShapeDtypeStruct((rows, streams * stream_width), jnp.bfloat16),
        *fixed,
        *lows,
        scratch=[
            pltpu.VMEM((rows, keys), jnp.bfloat16),
            pltpu.VMEM((count, weight_rows, keys), jnp.bfloat16),
        ],
    )


def shards(
    inputs,
    cotangent,
    frozen_key_weight,
    adapter_down_weight,
    adapter_up_weight,
    row_adapter_index,
    adapter_slot_index,
):
    tok_rows, feat_width = inputs.shape
    key_shard = cotangent.shape[1]
    owned, rank, _ = adapter_down_weight.shape
    slots = adapter_slot_index.shape[0]
    data_count, place = lax.axis_size("dp"), lax.axis_index("dp")
    down_rows = owned * rank
    key_at = lax.axis_index("fsdp") * key_shard

    up_own = lax.dynamic_slice_in_dim(adapter_up_weight, key_at, key_shard, 2)
    up_own = up_own.reshape(down_rows, key_shard)
    ups = [up_own] + turns(up_own, "dp")
    down_own = adapter_down_weight.reshape(down_rows, feat_width)
    packed = pack(down_own, frozen_key_weight)

    ids = row_adapter_index[:, 0]
    every = lax.broadcasted_iota(jnp.int32, (slots, tok_rows), 0)
    slot = jnp.sum(jnp.where(ids[None, :] == every, adapter_slot_index[:, None], 0), axis=0)
    slot = slot[None, :]

    def up_ways(step):
        ways = []
        for odd in (0, 1):
            ends = [i for i in range(data_count - step) if i // step % 2 == odd]

            def other(place, odd=odd):
                mine = lax.rem(lax.div(place, step), 2) == odd
                return jnp.where(mine, place + step, place - step)

            if ends:
                swaps = [(i, i + step) for i in ends] + [(i + step, i) for i in ends]
                ways.append((other, swaps))
        return ways

    def own_block(place):
        return place

    streams = range(len(packed))
    received = [[one, one] for one in packed]
    got, lows = [[one] for one in packed], [None for _ in streams]
    proj, back, exchanged, extras = None, None, [], [None, None]
    last = []
    waited = {step: [] for step in range(data_count + 3)}
    for step in range(1, data_count + 1):
        if step == 2:
            back = back_sum(slot, cotangent, ups, owned, rank)
            back = scaled_sum(back, "fsdp")
            cotangents = gathered(after(cotangent, back), "fsdp")
            waited[3] += [array for array, _ in cotangents]
        for stream in streams:
            sent = []
            for odd, other in enumerate(reversed(received[stream])):
                if step > 1:
                    other = after(other, last, waited[step] if stream == streams[-1] else [])
                if not only_blocks(step, odd):
                    extra = extras[odd] if stream == streams[-1] else None
                    other = message(
                        step, data_count, odd, stream, slot, back, inputs, other, extra, owned, rank
                    )
                sent.append(other)
            received[stream] = [
                lax.ppermute(sent[odd], "dp", pairs(data_count, odd)) for odd in (0, 1)
            ]
            if step == 1:
                continue
            pieces = after(got[stream], sent)
            if step == 2:
                proj, lows[stream], _ = use_pieces(
                    0, data_count, stream, slot, back, inputs, [packed[stream]], proj, None,
                    None, owned, rank,
                )
            merged = one_sided(data_count, step - 1)
            if stream == 0 or not merged:
                prior, described = None, []
            proj, lows[stream], share = use_pieces(
                step - 1, data_count, stream, slot, back, inputs, pieces, proj, lows[stream],
                prior, owned, rank,
            )
            last = [proj, lows[stream]]
            described += [(step - 1, stream, some) for some in ([odds] if merged else [[odd] for odd in odds])]
            prior = share
            if stream == streams[-1] or not merged:
                share = [share] + turns(share, "groups")
                waited[step + 1].append(share)
                exchanged.append((described, share))
        if step == data_count - 1:
            near = scaled_sum(proj, "fsdp")
            ways = sum([up_ways(away) for away in range(1, step)], [])
            targets = [own_block] + [other for other, _ in ways]
            up_own, *parts = up_parts(targets, slot, near, cotangent, owned, rank)
            extras = parts[:2]
            waiting = [(part, way) for part, (_, way) in zip(parts[2:], ways[2:])]
            proj = None
        odds = [odd for odd in (0, 1) if not only_sums(data_count, step, odd)]
        got = [[received[stream][odd] for odd in odds] for stream in streams]

    order = [entry for entry, _ in exchanged]
    parts = sum([share for _, share in exchanged], [])
    input_grad = finish(cotangents, frozen_key_weight, order, parts, lows)
    down_grad = None
    for stream in streams:
        if stream == streams[-1]:
            received[stream] = after(received[stream], input_grad)
        down_grad = own_sum(
            stream, slot, back, inputs, received[stream], down_grad, owned, rank
        )
        if stream == 0:
            others = [lax.ppermute(after(part, down_grad), "dp", way) for part, way in waiting]
            far = scaled_sum(after(proj, down_grad), "fsdp")
            ways = up_ways(data_count - 1)
            parts = up_parts([other for other, _ in ways], slot, far, cotangent, owned, rank)
            others += [lax.ppermute(part, "dp", way) for part, (_, way) in zip(parts, ways)]
    others = after(others, input_grad)
    up_grad = up_total(up_own, received[streams[-1]], others)
    return (
        input_grad,
        down_grad.reshape(owned, rank, feat_width),
        up_grad.reshape(owned, rank, key_shard),
    )


def solution(mesh):
    placed = (
        P(("groups", "dp"), "fsdp"),
        P(("groups", "dp"), "fsdp"),
        P(("fsdp", "dp"), None),
        P(("groups", "dp"), None, "fsdp"),
        P(("groups", "dp"), None, None),
        P(("groups", "dp"), None),
        P("groups"),
    )
    return jax.shard_map(
        shards,
        mesh=mesh,
        in_specs=placed,
        out_specs=(
            P(("groups", "dp"), "fsdp"),
            P(("groups", "dp"), None, "fsdp"),
            P(("groups", "dp"), None, "fsdp"),
        ),
        check_vma=False,
    )
```
